256 devices in a mesh: wide: 64 (over x, z_lo, y), narrow: 4 (over z_hi, core).
Axes of the slice: x: 4, y: 4, z: 8 (z_hi: 2, z_lo: 4; z = z_hi * 4 + z_lo), core: 2. Of those that a mesh axis runs over, the one named last changes fastest.
Arguments:
- frames_in: bfloat16 [128, 16, 16, 512], P('wide', None, None, 'narrow'), may hold values from -6 to 6
- conv_weight: bfloat16 [27, 512, 512], P(None, None, 'narrow'), may hold values from -0.0546875 to 0.0546875
- embed_weight: bfloat16 [512, 5120], P('narrow'), may hold values from -0.25 to 0.25
- action_table: float32 [8, 5120], replicated, may hold values from -3.5 to 3.5
- mask_embed: float32 [5120], replicated, may hold values from -3.5 to 3.5
- norm_gain: float32 [5120], replicated, may hold values from 0.25 to 1.75
- q_weight: bfloat16 [5120, 5120], P('wide', 'narrow'), may hold values from -0.048913987 to 0.048913987
- k_weight: bfloat16 [5120, 1024], P('wide', 'narrow'), may hold values from -0.048913987 to 0.048913987
- v_weight: bfloat16 [5120, 1024], P('wide', 'narrow'), may hold values from -0.078125 to 0.078125
- action_ids: int32 [128], P('wide'), may hold values from 0 to 7
- token_mask: int32 [128, 256], P('wide'), may hold values 0 or 1
Outputs:
- attended: bfloat16 [128, 4, 64, 5120], P(None, None, 'wide', 'narrow')
The draws below stay inside these ranges and needn't reach their ends.
All inputs are finite; a program needn't handle non-finite values. No bound on the sum of `token_mask` on one device may be relied on, other than what follows from the above.
Results may differ from the reference program's by a relative error of at most 0.015.
Values may be sent and summed in bfloat16 or wider, within the bound.
A program may use at most 128 MiB of HBM per device.

```python
import jax
import jax.numpy as jnp
from jax import lax

C = 512
D = 5120
HEAD = 128
QHEADS = 40
KVHEADS = 8
ACTIONS = 8
GRID = 16
FRAMES = 16
S = 256
NF = 128
CLIPS = 8
N_NARROW = 4


def draw_mask_embed(key, part):
    key = jax.random.fold_in(key, 3)
    noise = jax.random.normal(key, (D,), jnp.float32)
    result = noise
    return jnp.clip(result, -3.5, 3.5)


def draw_action_table(key, part):
    key = jax.random.fold_in(key, 5)
    result = jnp.clip(jax.random.normal(key, (ACTIONS, D), jnp.float32), -3.5, 3.5)
    return result


def draw_q_weight(key, part):
    key = jax.random.fold_in(key, 7)
    noise = jax.random.normal(key, (D, QHEADS * HEAD), jnp.float32)
    return (jnp.clip(noise, -3.5, 3.5) * D ** (-0.5)).astype(jnp.bfloat16)


def draw_k_weight(key, part):
    key = jax.random.fold_in(key, 9)
    noise = jax.random.normal(key, (D, KVHEADS * HEAD), jnp.float32)
    return (jnp.clip(noise, -3.5, 3.5) * D ** (-0.5)).astype(jnp.bfloat16)


def place_ends(values, rng, low, high):
    longest = values.shape.index(max(values.shape))
    spots = []
    for shift in (0, 1):
        where = [jax.random.randint(jax.random.fold_in(rng, axis), (), 0, length) for axis, length in enumerate(values.shape)]
        where[longest] = (where[longest] + shift) % values.shape[longest]
        spots.append(tuple(where))
    return values.at[spots[0]].set(low).at[spots[1]].set(high)


def levels(rng, shape, pieces, smallest, top_value):
    loudness, own = 1.0, jax.random.fold_in(rng, 6)
    for axis_at, shards_of in pieces:
        draws = jnp.exp(jax.random.uniform(jax.random.fold_in(own, axis_at), (shards_of,), jnp.float32, smallest / len(pieces), top_value / len(pieces)))
        loudness = loudness * jnp.repeat(draws, shape[axis_at] // shards_of).reshape([-1 if axis == axis_at else 1 for axis in range(len(shape))])
    return loudness


def scatter_about(stream_key, extent, width, bound, pieces=(), kind=jnp.bfloat16):
    values = width * jax.random.normal(stream_key, extent, jnp.float32)
    if pieces:
        values = values * levels(stream_key, extent, pieces, -0.22, 0.18)
    return jnp.clip(values, -bound, bound).astype(kind)


def setup_inputs(seed: int = 0) -> dict:
    key_list = jax.random.split(jax.random.key(seed), 12)
    frames_in = scatter_about(key_list[0], (NF, GRID, GRID, C), 1.0, 6.0, ((0, 64), (3, 4)))
    conv_weight = scatter_about(key_list[1], (27, C, C), (27 * C) ** -0.5, 0.0546875, ((2, 4),))
    embed_weight = scatter_about(key_list[2], (C, D), C ** -0.5, 0.25, ((0, 4),))
    action_table = draw_action_table(jax.random.fold_in(key_list[11], 71), 0)
    mask_embed = draw_mask_embed(jax.random.fold_in(key_list[11], 71), 0)
    norm_gain = jnp.clip(1.0 + 0.15 * jax.random.normal(key_list[5], (D,), jnp.float32), 0.25, 1.75)
    q_weight = draw_q_weight(jax.random.fold_in(key_list[11], 71), 0)
    k_weight = draw_k_weight(jax.random.fold_in(key_list[11], 71), 0)
    v_weight = scatter_about(key_list[8], (D, KVHEADS * HEAD), D ** -0.5, 0.078125, ((0, 64), (1, 4)))
    action_ids = place_ends(jax.random.randint(key_list[9], (NF,), 0, ACTIONS), jax.random.fold_in(key_list[9], 1), 0, ACTIONS - 1).astype(jnp.int32)
    token_mask = place_ends((jax.random.randint(key_list[10], (NF, S), 0, 2) < 1).astype(jnp.int32), jax.random.fold_in(key_list[10], 1), 0, 1)
    return {"frames_in": frames_in, "conv_weight": conv_weight, "embed_weight": embed_weight, "action_table": action_table, "mask_embed": mask_embed, "norm_gain": norm_gain, "q_weight": q_weight, "k_weight": k_weight, "v_weight": v_weight, "action_ids": action_ids, "token_mask": token_mask}


def encode_clip(block, conv_weight):
    padded = jnp.pad(block, ((0, 0), (1, 1), (1, 1), (0, 0)))
    taps = []
    for dt in range(3):
        for dh in range(3):
            for dw in range(3):
                taps.append(padded[dt:dt + FRAMES, dh:dh + GRID, dw:dw + GRID, :])
    columns = jnp.concatenate(taps, axis=-1).reshape(FRAMES * GRID * GRID, 27 * C)
    summed = jnp.dot(columns, conv_weight.reshape(27 * C, C), preferred_element_type=jnp.float32)
    return jax.nn.gelu(summed).astype(jnp.bfloat16)

def reference(frames_in, conv_weight, embed_weight, action_table, mask_embed, norm_gain, q_weight, k_weight, v_weight, action_ids, token_mask):
    stream = jnp.pad(frames_in, ((1, 1), (0, 0), (0, 0), (0, 0)))

    def encode_one(clip_index):
        block = lax.dynamic_slice_in_dim(stream, clip_index * FRAMES, FRAMES + 2, 0)
        return encode_clip(block, conv_weight)
    encoded = lax.map(encode_one, jnp.arange(CLIPS, dtype=jnp.int32))
    encoded = encoded.reshape(NF * S, C)
    width_block = C // N_NARROW
    emb_sum = jnp.zeros((NF * S, D), jnp.float32)
    for channel_block in range(N_NARROW):
        lower = channel_block * width_block
        upper = lower + width_block
        partial_sum = jnp.dot(encoded[:, lower:upper], embed_weight[lower:upper], preferred_element_type=jnp.float32)
        emb_sum = emb_sum + lax.optimization_barrier(partial_sum.astype(jnp.bfloat16)).astype(jnp.float32)
    emb_sum = emb_sum.reshape(NF, S, D)
    actions = action_table[action_ids]
    emb = jnp.where(token_mask[:, :, None] == 1, mask_embed[None, None, :], emb_sum) + actions[:, None, :]
    scale = lax.rsqrt(lax.optimization_barrier(jnp.mean(emb * emb, axis=-1, keepdims=True)) + 1e-05)
    normed = (emb * scale * norm_gain).astype(jnp.bfloat16).reshape(NF * S, D)
    queries = jnp.dot(normed, q_weight, preferred_element_type=jnp.float32).astype(jnp.bfloat16)
    keys = jnp.dot(normed, k_weight, preferred_element_type=jnp.float32).astype(jnp.bfloat16)
    values = jnp.dot(normed, v_weight, preferred_element_type=jnp.float32).astype(jnp.bfloat16)
    group = QHEADS // KVHEADS
    qs = queries.reshape(CLIPS, FRAMES, S, KVHEADS, group, HEAD).astype(jnp.float32)
    ks = keys.reshape(CLIPS, FRAMES, S, KVHEADS, HEAD).astype(jnp.float32)
    vs = values.reshape(CLIPS, FRAMES, S, KVHEADS, HEAD).astype(jnp.float32)
    scores = jnp.einsum('cfrkgd,ctrkd->crkgft', qs, ks) * (1.0 / HEAD ** 0.5)
    causal = jnp.arange(FRAMES)[:, None] >= jnp.arange(FRAMES)[None, :]
    scores = jnp.where(causal, scores, -1e+30)
    top = lax.optimization_barrier(jnp.max(scores, axis=-1, keepdims=True))
    expd = jnp.exp(scores - top)
    probs = (expd / lax.optimization_barrier(jnp.sum(expd, axis=-1, keepdims=True))).astype(jnp.bfloat16).astype(jnp.float32)
    attended = jnp.einsum('crkgft,ctrkd->cfrkgd', probs, vs).astype(jnp.bfloat16)
    return attended.reshape(NF, N_NARROW, S // N_NARROW, QHEADS * HEAD)
```

```python
import jax
import jax.numpy as jnp
from jax import lax
from jax.experimental import pallas as pl
from jax.experimental.pallas import tpu as pltpu
from jax.sharding import PartitionSpec as P

MESH = pl.DeviceIdType.MESH
F32 = jnp.float32
BF16 = jnp.bfloat16
HEAD = 128
ROWS = 144


def exchange_kernel(
    fr, cw_hbm, ew, sb, qw, kw, vw, gw, xx,
    ph, ex, kf, nr,
    cw, xr, sh, acc, ge, pieces, qx, qe, ws, wb, fb, ka, kr, nb,
    cw_sem, ssem, rsem, psend, precv,
):
    w = lax.axis_index("wide")
    n = lax.axis_index("narrow")
    x, zl, y = w // 16, (w // 4) % 4, w % 4
    zh, c = n // 2, n % 2
    p = x * 4 + y
    n1, n2 = zh * 2 + (1 - c), (1 - zh) * 2 + c
    m, m1, m2 = c * 2 + zh, (1 - c) * 2 + zh, c * 2 + (1 - zh)
    wnext, wprev = (w + 1) % 64, (w + 63) % 64

    def zpeer(d):
        z = (zl + d) % 4
        return z, x * 16 + z * 4 + y

    def ppeer(d):
        px, py = (x + d // 4) % 4, (y + d % 4) % 4
        return px * 4 + py, px * 16 + zl * 4 + py

    def cp(src, dst, slot, dev):
        return pltpu.make_async_remote_copy(
            src_ref=src, dst_ref=dst, send_sem=ssem.at[slot], recv_sem=rsem.at[slot],
            device_id=dev, device_id_type=MESH,
        )

    def pcp(src, dst, group, d, dev):
        return pltpu.make_async_remote_copy(
            src_ref=src, dst_ref=dst, send_sem=psend.at[group, d], recv_sem=precv.at[group, d],
            device_id=dev, device_id_type=MESH,
        )

    load = pltpu.make_async_copy(cw_hbm, cw, cw_sem)
    load.start()

    barrier = pltpu.get_barrier_semaphore()

    def greet(dev):
        pl.semaphore_signal(barrier, inc=1, device_id=dev, device_id_type=MESH)

    for dev in ((w, n1), (w, n2), (wnext, n), (wprev, n)):
        greet(dev)
    for d in range(1, 4):
        greet((zpeer(d)[1], n))

    def greet_plane(d, carry):
        greet((ppeer(d)[1], n))
        return carry

    lax.fori_loop(1, 16, greet_plane, 0)

    for t in range(14):
        source, col = (qw, t) if t < 10 else ((kw, t - 10) if t < 12 else (vw, t - 12))
        ws[t, 0:80, :] = (source[:, col * 128:col * 128 + 128].astype(F32) * gw[...]).astype(BF16)
    for t in range(14, 16):
        ws[t, 0:80, :] = jnp.zeros((80, 128), BF16)
    for t in range(16):
        wb[t, 80:128, :] = jnp.zeros((48, 128), BF16)
    wb[p, 0:80, :] = ws[p, 0:80, :]
    fb[p, m] = ew[...]
    xr[n, 1:3] = fr[...]
    qx[zl] = xx[zl]
    pl.semaphore_wait(barrier, 22)

    e_opp = cp(ew, fb.at[p, m], 11, (w, n2))
    e_opp.start()
    f_opp = cp(fr, xr.at[n, pl.ds(1, 2)], 1, (w, n2))
    f_opp.start()
    h_next = cp(fr.at[1], xr.at[n, 0], 3, (wnext, n))
    h_next.start()
    h_prev = cp(fr.at[0], xr.at[n, 3], 4, (wprev, n))
    h_prev.start()
    f_sib = cp(fr, xr.at[n, pl.ds(1, 2)], 0, (w, n1))
    f_sib.start()

    def w_copy(d):
        there, dev = ppeer(d)
        return pcp(ws.at[there, pl.ds(0, 80)], wb.at[p, pl.ds(0, 80)], 0, d, (dev, n))

    def plane(make, op):
        def body(d, carry):
            op(make(d))
            return carry
        lax.fori_loop(1, 16, body, 0)

    plane(w_copy, lambda k: k.start())
    x_copies = []
    for d in range(1, 4):
        there, dev = zpeer(d)
        x_copies.append(cp(xx.at[there], qx.at[zl], 12 + d, (dev, n)))
        x_copies[-1].start()

    e_opp.wait_recv()

    def e_copy(d):
        there, dev = ppeer(d)
        return pcp(fb.at[p, pl.ds(2 * c, 2)], fb.at[p, pl.ds(2 * c, 2)], 1, d, (dev, n))

    plane(e_copy, lambda k: k.start())

    for k in x_copies:
        k.wait_recv()

    def x_copy(d):
        there, dev = ppeer(d)
        return pcp(qx.at[:, there], ex.at[x, :, y], 2, d, (dev, n))

    plane(x_copy, lambda k: k.start())
    for z in range(4):
        ex[x, z, y] = qx[z, p]

    f_opp.wait_recv()
    f_fwd = cp(xr.at[n2, pl.ds(1, 2)], xr.at[n2, pl.ds(1, 2)], 2, (w, n1))
    h2_next = cp(xr.at[n2, 2], xr.at[n2, 0], 5, (wnext, n))
    h2_prev = cp(xr.at[n2, 1], xr.at[n2, 3], 6, (wprev, n))
    h2_next.start()
    h2_prev.start()
    f_fwd.start()
    h_next.wait_recv()
    h_prev.wait_recv()
    s_copies = [cp(xr.at[n, 0], xr.at[n, 0], 7, (w, n1)), cp(xr.at[n, 3], xr.at[n, 3], 8, (w, n1))]
    for k in s_copies:
        k.start()

    plane(e_copy, lambda k: k.wait_recv())
    e_sib = cp(fb.at[:, pl.ds(2 * c, 2)], fb.at[:, pl.ds(2 * c, 2)], 12, (w, n1))
    e_sib.start()

    h2_next.wait_recv()
    h2_prev.wait_recv()
    s2_copies = [cp(xr.at[n2, 0], xr.at[n2, 0], 9, (w, n1)), cp(xr.at[n2, 3], xr.at[n2, 3], 10, (w, n1))]
    for k in s2_copies:
        k.start()

    plane(w_copy, lambda k: k.wait_recv())
    e_sib.wait_recv()

    ka[...] = jnp.zeros(ka.shape, F32)

    def tile(transposed):
        def body(i, carry):
            first, second = 2 * i, 2 * i + 1
            lhs = jnp.concatenate([fb[first].reshape(512, 128), fb[second].reshape(512, 128)], axis=1)
            small = jnp.concatenate([sb[first], sb[second]], axis=1)
            if transposed:
                rhs = jnp.concatenate([fb[first, m], fb[second, m]], axis=1)
                dims = (((1,), (1,)), ((), ()))
            else:
                rhs = jnp.concatenate([wb[first], wb[second]], axis=0)
                dims = (((1,), (0,)), ((), ()))
            big = lax.dot_general(lhs, rhs, dims, preferred_element_type=F32)
            both = lax.dot_general(small, rhs, dims, preferred_element_type=F32)
            for q in range(3):
                ka[q] += big[q * ROWS:q * ROWS + ROWS]
            ka[3, 0:80] += big[432:512]
            ka[3, 80:96] += both[0:16] + both[16:32]
            return carry
        lax.fori_loop(0, 8, body, 0)

    @pl.when(p < 14)
    def _():
        tile(False)

    @pl.when(p >= 14)
    def _():
        tile(True)

    k_copies = []
    for d in range(1, 4):
        there, dev = zpeer(d)
        k_copies.append(cp(ka.at[there], kr.at[zl], 15 + d, (dev, n)))
        k_copies[-1].start()
    kr[zl] = ka[zl]

    f_sib.wait_recv()
    f_fwd.wait_recv()
    for k in s_copies + s2_copies:
        k.wait_recv()
    zero_row = jnp.zeros((4, 1, 16, 512), BF16)
    for dw in range(3):
        sh[dw, :, 0:1] = zero_row
        sh[dw, :, 17:18] = zero_row
    column = lax.broadcasted_iota(jnp.int32, (256, 128), 0) % 16

    def shift(slot, carry):
        edge = ((w == 0) & (slot == 0)) | ((w == 63) & (slot == 3))
        keep = jnp.where(edge, 0.0, 1.0)
        for b in range(4):
            block = xr[b, slot].astype(F32) * keep
            lanes = slice(b * 128, b * 128 + 128)
            left = jnp.where(column == 0, 0.0, pltpu.roll(block, 1, 0))
            right = jnp.where(column == 15, 0.0, pltpu.roll(block, 255, 0))
            for dw, part in enumerate((left, block, right)):
                sh[dw, slot, 1:17, :, lanes] = part.astype(BF16).reshape(16, 16, 128)
        return carry

    lax.fori_loop(0, 4, shift, 0)
    load.wait()
    acc[...] = jnp.zeros(acc.shape, F32)

    def tap(i, carry):
        dt, dh = i // 3, i % 3
        total = acc[...]
        for dw in range(3):
            lhs = sh[dw, pl.ds(dt, 2), pl.ds(dh, 16)].reshape(512, 512)
            total = total + jnp.dot(lhs, cw[i * 3 + dw], preferred_element_type=F32)
        acc[...] = total
        return carry

    lax.fori_loop(0, 9, tap, 0)
    ge[...] = jax.nn.gelu(acc[...])
    for z in range(4):
        for k in range(16):
            where = (k // 4) * 16 + z * 4 + k % 4
            pieces[z, k] = ge[pl.ds(where, 8, stride=64), :].astype(BF16)
    qe[zl] = pieces[zl]
    p_copies = []
    for d in range(1, 4):
        there, dev = zpeer(d)
        p_copies.append(cp(pieces.at[there], qe.at[zl], 18 + d, (dev, n)))
        p_copies[-1].start()

    for k in k_copies:
        k.wait_recv()
    summed = (kr[0] + kr[1]) + (kr[2] + kr[3])
    high = summed.astype(BF16)
    low = summed - high.astype(F32)
    kf[p, zl] = jnp.where(p == 15, low, high.astype(F32)).astype(BF16)
    g_copies = []
    for d in range(1, 4):
        there, dev = zpeer(d)
        g_copies.append(cp(kf.at[p, zl], kf.at[p, zl], 21 + d, (dev, n)))
        g_copies[-1].start()

    for k in p_copies:
        k.wait_recv()

    def p_copy(d):
        there, dev = ppeer(d)
        return pcp(qe.at[:, there], ph.at[m, x, :, y], 3, d, (dev, n))

    plane(p_copy, lambda k: k.start())
    for z in range(4):
        ph[m, x, z, y] = qe[z, p]

    for k in g_copies:
        k.wait_recv()

    def k_copy(d):
        there, dev = ppeer(d)
        return pcp(kf.at[p], kf.at[p], 4, d, (dev, n))

    plane(k_copy, lambda k: k.start())

    plane(p_copy, lambda k: k.wait_recv())
    t_opp = cp(ph.at[m], ph.at[m], 25, (w, n2))
    t_sib = cp(ph.at[m], ph.at[m], 26, (w, n1))
    t_opp.start()
    t_sib.start()
    t_opp.wait_recv()
    t_fwd = cp(ph.at[m2], ph.at[m2], 27, (w, n1))
    t_fwd.start()
    t_sib.wait_recv()
    t_fwd.wait_recv()
    plane(x_copy, lambda k: k.wait_recv())
    plane(k_copy, lambda k: k.wait_recv())

    extra = ex[...].reshape(512, 128)
    open_rows = 1.0 - extra[:, 8:9].astype(F32)
    y_sum = jnp.zeros((512, 128), F32)
    for t in (14, 15):
        g = kf[t].reshape(576, 128)
        for b in range(4):
            e = (ph[b].reshape(512, 128).astype(F32) * open_rows).astype(BF16)
            y_sum = y_sum + jnp.dot(e, g[b * 128:b * 128 + 128], preferred_element_type=F32)
        g_small = jnp.concatenate([g[512:576], jnp.zeros((64, 128), BF16)], axis=0)
        y_sum = y_sum + 2.0 * jnp.dot(extra, g_small, preferred_element_type=F32)
    mine = y_sum * (ph[m].reshape(512, 128).astype(F32) * open_rows)
    nb[0] = lax.dot_general(
        jnp.ones((8, 128), F32), mine, (((1,), (1,)), ((), ())),
        precision=lax.Precision.HIGHEST, preferred_element_type=F32,
    )
    n_opp = cp(nb.at[0], nb.at[1], 28, (w, n2))
    n_opp.start()
    n_opp.wait_recv()
    nb[2] = nb[0] + nb[1]
    n_sib = cp(nb.at[2], nb.at[3], 29, (w, n1))
    n_sib.start()
    n_sib.wait_recv()
    nr[...] = nb[2] + nb[3]

    for k in [e_opp, f_opp, h_next, h_prev, f_sib, f_fwd, h2_next, h2_prev, e_sib, t_opp, t_sib, t_fwd, n_opp, n_sib]:
        k.wait_send()
    for k in x_copies + s_copies + s2_copies + k_copies + p_copies + g_copies:
        k.wait_send()
    for make in (w_copy, e_copy, x_copy, p_copy, k_copy):
        plane(make, lambda k: k.wait_send())


def attend_kernel(ph, ex, kf, nr, base, out, qkv):
    extra = ex[...].reshape(512, 128)
    wide_extra = extra.astype(F32)
    masked = wide_extra[:, 8:9]
    e = jnp.concatenate(
        [(ph[b].reshape(512, 128).astype(F32) * (1.0 - masked)).astype(BF16) for b in range(4)] + [extra], axis=1
    )
    squares = jnp.transpose(nr[...])[:, 0:1]
    squares = squares + jnp.sum(wide_extra * (base[0:1, :] + masked * base[1:2, :]), axis=1, keepdims=True)
    scale = lax.rsqrt(jnp.maximum(squares, 0.0) * (1.0 / 5120.0) + 1e-05)
    pad = jnp.zeros((64, 256), BF16)
    for j in range(7):
        rhs = jnp.concatenate([kf[2 * j].reshape(576, 128), kf[2 * j + 1].reshape(576, 128)], axis=1)
        rhs = jnp.concatenate([rhs, pad], axis=0)
        qkv[:, j * 256:j * 256 + 256] = (
            jnp.dot(e, rhs, preferred_element_type=F32) * scale
        ).astype(BF16)
    row = lax.broadcasted_iota(jnp.int32, (640, 128), 0) % 128
    col = lax.broadcasted_iota(jnp.int32, (640, 128), 1)
    keep = (row % 4 == col % 4) & (row // 64 == col // 64) & (col <= row)

    def group(i, carry):
        rows = pl.ds(pl.multiple_of(i * 128, 128), 128)
        for h in range(2):
            q = jnp.concatenate(
                [qkv[rows, (h * 5 + g) * 128:(h * 5 + g) * 128 + 128] for g in range(5)], axis=0
            )
            k = qkv[rows, 1280 + h * 128:1408 + h * 128]
            v = qkv[rows, 1536 + h * 128:1664 + h * 128]
            s = lax.dot_general(q, k, (((1,), (1,)), ((), ())), preferred_element_type=F32) * (1.0 / HEAD**0.5)
            s = jnp.where(keep, s, -1e30)
            top = jnp.max(s, axis=1, keepdims=True)
            exps = jnp.exp(s - top)
            probs = (exps / jnp.sum(exps, axis=1, keepdims=True)).astype(BF16)
            mixed = jnp.dot(probs, v, preferred_element_type=F32).astype(BF16)
            for g in range(5):
                out[rows, (h * 5 + g) * 128:(h * 5 + g) * 128 + 128] = mixed[g * 128:g * 128 + 128]
        return carry

    lax.fori_loop(0, 4, group, 0)


VMEM = pl.BlockSpec(memory_space=pltpu.VMEM)


def shards(
    frames_in, conv_weight, embed_weight, action_table, mask_embed, norm_gain,
    q_weight, k_weight, v_weight, action_ids, token_mask,
):
    w = lax.axis_index("wide")
    zl = (w // 4) % 4
    ew = jnp.pad(lax.dynamic_slice_in_dim(embed_weight, w * 80, 80, 1), ((0, 0), (0, 48)))
    gw = jnp.broadcast_to(lax.dynamic_slice_in_dim(norm_gain, w * 80, 80, 0)[:, None], (80, 128))
    small = jnp.concatenate([action_table, mask_embed[None], jnp.zeros((7, 5120), F32)], axis=0)
    small = lax.dynamic_index_in_dim(small.reshape(16, 4, 4, 320), zl, 2, keepdims=False)
    high = lax.reduce_precision(small, 8, 7)
    both = jnp.concatenate([high, small - high], axis=0).astype(BF16)
    sb = jnp.transpose(both.reshape(32, 4, 4, 80), (1, 2, 0, 3)).reshape(16, 32, 80)
    sb = jnp.pad(sb, ((0, 0), (0, 0), (0, 48)))
    lane = jnp.arange(128, dtype=jnp.int32)
    onehot = (action_ids[:, None] == lane[None, :]).astype(BF16)
    tokens = jnp.transpose(token_mask.reshape(2, 4, 4, 4, 4), (3, 2, 4, 0, 1)).reshape(4, 16, 8)
    mask_lane = (lane == 8).astype(BF16)
    xx = jnp.repeat(onehot, 4, axis=0)[None, None] + (tokens == 1).astype(BF16)[..., None] * mask_lane
    squares = jnp.sum(action_table * action_table, axis=1)
    cross = 2.0 * jnp.sum(action_table * mask_embed[None], axis=1) + jnp.sum(mask_embed * mask_embed)
    base = jnp.pad(jnp.stack([squares, cross]), ((0, 6), (0, 120)))

    ph, ex, kf, nr = pl.pallas_call(
        exchange_kernel,
        out_shape=(
            jax.ShapeDtypeStruct((4, 4, 4, 4, 8, 128), BF16),
            jax.ShapeDtypeStruct((4, 4, 4, 8, 128), BF16),
            jax.ShapeDtypeStruct((16, 4, ROWS, 128), BF16),
            jax.ShapeDtypeStruct((8, 512), F32),
        ),
        in_specs=[VMEM, pl.BlockSpec(memory_space=pl.ANY)] + [VMEM] * 7,
        out_specs=(VMEM,) * 4,
        scratch_shapes=[
            pltpu.VMEM((27, 512, 128), BF16),
            pltpu.VMEM((4, 4, 256, 128), BF16),
            pltpu.VMEM((3, 4, 18, 16, 512), BF16),
            pltpu.VMEM((512, 128), F32),
            pltpu.VMEM((512, 128), F32),
            pltpu.VMEM((4, 16, 8, 128), BF16),
            pltpu.VMEM((4, 16, 8, 128), BF16),
            pltpu.VMEM((4, 16, 8, 128), BF16),
            pltpu.VMEM((16, 80, 128), BF16),
            pltpu.VMEM((16, 128, 128), BF16),
            pltpu.VMEM((16, 4, 128, 128), BF16),
            pltpu.VMEM((4, ROWS, 128), F32),
            pltpu.VMEM((4, ROWS, 128), F32),
            pltpu.VMEM((4, 8, 512), F32),
            pltpu.SemaphoreType.DMA,
            pltpu.SemaphoreType.DMA((30,)),
            pltpu.SemaphoreType.DMA((30,)),
            pltpu.SemaphoreType.DMA((5, 16)),
            pltpu.SemaphoreType.DMA((5, 16)),
        ],
        compiler_params=pltpu.CompilerParams(
            collective_id=0, has_side_effects=True, vmem_limit_bytes=40 * 1024 * 1024
        ),
        name="exchange",
    )(frames_in.reshape(2, 256, 128), conv_weight, ew, sb, q_weight, k_weight, v_weight, gw, xx)

    attended = pl.pallas_call(
        attend_kernel,
        out_shape=jax.ShapeDtypeStruct((512, 1280), BF16),
        in_specs=[VMEM] * 5,
        out_specs=VMEM,
        scratch_shapes=[pltpu.VMEM((512, 1792), BF16)],
        compiler_params=pltpu.CompilerParams(vmem_limit_bytes=40 * 1024 * 1024),
        name="attend",
    )(ph, ex, kf, nr, base)
    return attended.reshape(128, 4, 1, 1280)


def solution(mesh):
    return jax.shard_map(
        shards,
        mesh=mesh,
        in_specs=(
            P("wide", None, None, "narrow"),
            P(None, None, "narrow"),
            P("narrow", None),
            P(),
            P(),
            P(),
            P("wide", "narrow"),
            P("wide", "narrow"),
            P("wide", "narrow"),
            P("wide"),
            P("wide", None),
        ),
        out_specs=P(None, None, "wide", "narrow"),
        check_vma=False,
    )
```

```python
import jax
import jax.numpy as jnp
from jax import lax
from jax.experimental import pallas as pl
from jax.experimental.pallas import tpu as pltpu
from jax.sharding import PartitionSpec as P

MESH = pl.DeviceIdType.MESH
F32 = jnp.float32
BF16 = jnp.bfloat16
HEAD = 128
ROWS = 144
WIN = 384
DEPTH = 4 * WIN
NT = (((1,), (1,)), ((), ()))


def whole_kernel(
    ids, fr_hbm, cw_hbm, ew_hbm, at_hbm, me_hbm, ga_hbm, qw_hbm, kw_hbm, vw_hbm, tm_hbm,
    out,
    fr, at, me, ga, qw, kw, vw, tm, gc, cw, xr, sh, acc, ge, pieces, qe, xx, qx, ex, ph, ws, wb, fb, sb, gp, gr, gl, ka, kr, kf, nb, qkv,
    lsem, ssem, rsem, psend, precv,
):
    w = lax.axis_index("wide")
    n = lax.axis_index("narrow")
    x, zl, y = w // 16, (w // 4) % 4, w % 4
    zh, c = n // 2, n % 2
    p = x * 4 + y
    n1, n2 = zh * 2 + (1 - c), (1 - zh) * 2 + c
    m, m1, m2 = c * 2 + zh, (1 - c) * 2 + zh, c * 2 + (1 - zh)
    odd = zl % 2
    start = (zl * 320 // 128) * 128

    def at_plane(px, py):
        return px * 16 + zl * 4 + py

    def zpeer(d):
        z = (zl + d) % 4
        return z, (x * 16 + z * 4 + y, n)

    def ppeer(d):
        px, py = (x + d // 4) % 4, (y + d % 4) % 4
        return px * 4 + py, (at_plane(px, py), n)

    sib, opp = (w, n1), (w, n2)
    wnext, wprev = ((w + 1) % 64, n), ((w + 63) % 64, n)
    xa, xb = (x + 1) % 4, (x + 3) % 4
    ya, yb = (y + 1) % 4, (y + 3) % 4
    xnext, xprev = (at_plane(xa, y), n), (at_plane(xb, y), n)
    ynext, yprev = (at_plane(x, ya), n), (at_plane(x, yb), n)

    def cp(src, dst, slot, dev):
        return pltpu.make_async_remote_copy(
            src_ref=src, dst_ref=dst, send_sem=ssem.at[slot], recv_sem=rsem.at[slot],
            device_id=dev, device_id_type=MESH,
        )

    started = []

    def go(src, dst, slot, dev):
        k = cp(src, dst, slot, dev)
        k.start()
        started.append(k)
        return k

    def pcp(src, dst, group, d, dev):
        return pltpu.make_async_remote_copy(
            src_ref=src, dst_ref=dst, send_sem=psend.at[group, d], recv_sem=precv.at[group, d],
            device_id=dev, device_id_type=MESH,
        )

    def plane(make, op):
        def body(d, carry):
            op(make(d))
            return carry
        lax.fori_loop(1, 16, body, 0)

    def begin(k):
        k.start()

    def arrive(k):
        k.wait_recv()

    e_loads = []
    for i in range(4):
        e_loads.append(pltpu.make_async_copy(
            ew_hbm.at[:, :, pl.ds(pl.multiple_of(1280 * i + start, 128), WIN)],
            fb.at[pl.ds(m * 16, 16), :, pl.ds(WIN * i, WIN)],
            lsem.at[i],
        ))
        e_loads[-1].start()
    loads = []
    for i, (src, dst) in enumerate((
        (fr_hbm, fr), (ga_hbm, ga), (qw_hbm, qw), (kw_hbm, kw), (vw_hbm, vw), (at_hbm, at), (me_hbm, me), (tm_hbm, tm),
        (cw_hbm, cw),
    )):
        loads.append(pltpu.make_async_copy(src, dst, lsem.at[4 + i]))
        loads[-1].start()
    taps = loads.pop()

    barrier = pltpu.get_barrier_semaphore()

    def greet(dev):
        pl.semaphore_signal(barrier, inc=1, device_id=dev, device_id_type=MESH)

    for dev in (sib, opp, wnext, wprev, zpeer(1)[1], zpeer(2)[1], zpeer(3)[1]):
        greet(dev)

    def greet_plane(d, carry):
        greet(ppeer(d)[1])
        return carry

    lax.fori_loop(1, 16, greet_plane, 0)

    for k in loads:
        k.wait()
    cols = pl.ds(pl.multiple_of(1280 * x + start, 128), WIN)
    gain = jnp.broadcast_to(ga[:, cols], (8, WIN))
    for i in range(3):
        gc[i * 128:i * 128 + 128] = jnp.transpose(
            jnp.concatenate([gain[:, i * 128:i * 128 + 128], jnp.zeros((120, 128), F32)], axis=0))
    gain = gc[pl.ds(pl.multiple_of(odd * 64 + y * 80, 8), 80), :][:, 0:1]
    for t in range(14):
        source, col = (qw, t) if t < 10 else ((kw, t - 10) if t < 12 else (vw, t - 12))
        ws[t] = (source[:, col * 128:col * 128 + 128].astype(F32) * gain).astype(BF16)
    for t in range(14, 16):
        ws[t] = jnp.zeros((80, 128), BF16)
    for i in range(4):
        wb[pl.ds(pl.multiple_of(i * WIN + (1 - odd) * 320, 16), 64), :] = jnp.zeros((64, 128), BF16)

    def w_rows(px, py):
        return pl.ds(pl.multiple_of(px * WIN + odd * 64 + py * 80, 16), 80)

    wb[w_rows(x, y), :] = ws[p]
    xr[n, 1:3] = fr[...]

    pl.semaphore_wait(barrier, 22)

    for k in e_loads:
        k.wait()
    e_opp = go(fb.at[m * 16 + p], fb.at[m * 16 + p], 11, opp)
    f_opp = go(fr, xr.at[n, pl.ds(1, 2)], 1, opp)
    h_next = go(fr.at[1], xr.at[n, 0], 3, wnext)
    h_prev = go(fr.at[0], xr.at[n, 3], 4, wprev)
    f_sib = go(fr, xr.at[n, pl.ds(1, 2)], 0, sib)
    e_sib = go(fb.at[pl.ds(m * 16, 16)], fb.at[pl.ds(m * 16, 16)], 12, sib)

    def w_copy(d):
        there, dev = ppeer(d)
        return pcp(ws.at[there], wb.at[w_rows(x, y)], 0, d, dev)

    plane(w_copy, begin)

    lane = lax.broadcasted_iota(jnp.int32, (4, 128), 1)
    onehot = jnp.concatenate([jnp.where(lane == ids[f], 1.0, 0.0) for f in range(2)], axis=0)
    lane8 = jnp.where(lax.broadcasted_iota(jnp.int32, (8, 128), 1) == 8, 1.0, 0.0)
    masks = jnp.concatenate(
        [tm[f:f + 1, i * 64:i * 64 + 64] for f in range(2) for i in range(4)], axis=0)
    masks = jnp.where(masks == 1, 1.0, 0.0)
    for z in range(4):
        for k in range(16):
            where = (k // 4) * 16 + z * 4 + k % 4
            xx[z, k] = (onehot + masks[:, where:where + 1] * lane8).astype(BF16)
    qx[zl] = xx[zl]
    x_copies = []
    for d in range(1, 4):
        there, dev = zpeer(d)
        x_copies.append(go(xx.at[there], qx.at[zl], 12 + d, dev))

    for i in range(4):
        cols = pl.ds(pl.multiple_of(1280 * i + start, 128), WIN)
        rows = jnp.concatenate([at[:, cols], me[:, cols], jnp.zeros((7, WIN), F32)], axis=0)
        high = rows.astype(BF16)
        sb[0:16, i * WIN:i * WIN + WIN] = high
        sb[16:32, i * WIN:i * WIN + WIN] = (rows - high.astype(F32)).astype(BF16)
    table = at[...]
    masked_row = me[...]
    squares0 = jnp.sum(table * table, axis=1, keepdims=True)
    squares1 = 2.0 * jnp.sum(table * masked_row, axis=1, keepdims=True) + jnp.sum(masked_row * masked_row)
    empty = jnp.zeros((120, 128), F32)
    base0 = jnp.transpose(jnp.concatenate([jnp.broadcast_to(squares0, (8, 128)), empty], axis=0))[0:1, :]
    base1 = jnp.transpose(jnp.concatenate([jnp.broadcast_to(squares1, (8, 128)), empty], axis=0))[0:1, :]

    e_opp.wait_recv()

    def e_copy(d):
        there, dev = ppeer(d)
        return pcp(fb.at[m2 * 16 + p], fb.at[m2 * 16 + p], 1, d, dev)

    plane(e_copy, begin)

    for k in x_copies:
        k.wait_recv()

    def x_copy(d):
        there, dev = ppeer(d)
        return pcp(qx.at[:, there], ex.at[x, :, y], 2, d, dev)

    plane(x_copy, begin)
    for z in range(4):
        ex[x, z, y] = qx[z, p]

    f_opp.wait_recv()
    h2_next = go(xr.at[n2, 2], xr.at[n2, 0], 5, wnext)
    h2_prev = go(xr.at[n2, 1], xr.at[n2, 3], 6, wprev)
    f_fwd = go(xr.at[n2, pl.ds(1, 2)], xr.at[n2, pl.ds(1, 2)], 2, sib)
    h_next.wait_recv()
    h_prev.wait_recv()
    s_copies = [go(xr.at[n, 0], xr.at[n, 0], 7, sib), go(xr.at[n, 3], xr.at[n, 3], 8, sib)]

    plane(e_copy, arrive)
    e_fwd = go(fb.at[pl.ds(m2 * 16, 16)], fb.at[pl.ds(m2 * 16, 16)], 10, sib)

    h2_next.wait_recv()
    h2_prev.wait_recv()
    s_copies += [go(xr.at[n2, 0], xr.at[n2, 0], 9, sib), go(xr.at[n2, 3], xr.at[n2, 3], 25, sib)]

    plane(w_copy, arrive)
    e_sib.wait_recv()
    e_fwd.wait_recv()

    where = lax.broadcasted_iota(jnp.int32, (128, DEPTH), 1) % WIN
    valid = jnp.where(odd == 1, jnp.where(where >= 64, 1.0, 0.0), jnp.where(where < 320, 1.0, 0.0))
    block = (fb[pl.ds(m * 16, 16)].reshape(128, DEPTH).astype(F32) * valid).astype(BF16)
    gp[0:32] = lax.dot_general(
        fb[pl.ds(p * 4, 4)].reshape(32, DEPTH), block, NT, preferred_element_type=F32)
    both = lax.dot_general(sb[...], block, NT, preferred_element_type=F32)
    gp[32:48] = both[0:16] + both[16:32]
    g_copies = []
    for d in range(1, 4):
        there, dev = zpeer(d)
        g_copies.append(go(gp, gr.at[zl], 15 + d, dev))
    gr[zl] = gp[...]

    for b in range(4):
        part = jnp.dot(fb[b * 16:b * 16 + 16].reshape(128, DEPTH), wb[...], preferred_element_type=F32)
        ka[b * 128:b * 128 + 128] = part.astype(BF16)
    both = jnp.dot(sb[...], wb[...], preferred_element_type=F32)
    ka[512:528] = (both[0:16] + both[16:32]).astype(BF16)
    ka[528:576] = jnp.zeros((48, 128), BF16)

    def quarter(z):
        return pl.ds(pl.multiple_of(z * ROWS, 16), ROWS)

    k_copies = []
    for d in range(1, 4):
        there, dev = zpeer(d)
        k_copies.append(go(ka.at[quarter(there)], kr.at[zl], 18 + d, dev))
    kr[zl] = ka[quarter(zl), :]

    f_sib.wait_recv()
    f_fwd.wait_recv()
    for k in s_copies:
        k.wait_recv()
    zero_row = jnp.zeros((4, 1, 16, 512), BF16)
    for dw in range(3):
        sh[dw, :, 0:1] = zero_row
        sh[dw, :, 17:18] = zero_row
    column = lax.broadcasted_iota(jnp.int32, (256, 128), 0) % 16

    def shift(slot, carry):
        edge = ((w == 0) & (slot == 0)) | ((w == 63) & (slot == 3))
        keep = jnp.where(edge, 0.0, 1.0)
        for b in range(4):
            cells = xr[b, slot].astype(F32) * keep
            lanes = slice(b * 128, b * 128 + 128)
            left = jnp.where(column == 0, 0.0, pltpu.roll(cells, 1, 0))
            right = jnp.where(column == 15, 0.0, pltpu.roll(cells, 255, 0))
            for dw, part in enumerate((left, cells, right)):
                sh[dw, slot, 1:17, :, lanes] = part.astype(BF16).reshape(16, 16, 128)
        return carry

    lax.fori_loop(0, 4, shift, 0)

    for k in g_copies:
        k.wait_recv()
    gsum = (gr[0] + gr[1]) + (gr[2] + gr[3])
    gl[pl.ds(pl.multiple_of(p * 32, 8), 32), :] = gsum[0:32]
    gl[512:528] = gsum[32:48]

    def g_rows():
        return pl.ds(pl.multiple_of(p * 32, 8), 32)

    def g_copy(d):
        there, dev = ppeer(d)
        return pcp(gl.at[g_rows()], gl.at[g_rows()], 3, d, dev)

    plane(g_copy, begin)
    for k in k_copies:
        k.wait_recv()
    ksum = (kr[0].astype(F32) + kr[1].astype(F32)) + (kr[2].astype(F32) + kr[3].astype(F32))
    kf[x, y, quarter(zl), :] = ksum.astype(BF16)
    q_copies = []
    for d in range(1, 4):
        there, dev = zpeer(d)
        q_copies.append(go(kf.at[x, y, quarter(zl)], kf.at[x, y, quarter(zl)], 21 + d, dev))

    taps.wait()
    acc[...] = jnp.zeros(acc.shape, F32)

    def tap(i, carry):
        dt, dh = i // 3, i % 3
        total = acc[...]
        for dw in range(3):
            lhs = sh[dw, pl.ds(dt, 2), pl.ds(dh, 16)].reshape(512, 512)
            total = total + jnp.dot(lhs, cw[i * 3 + dw], preferred_element_type=F32)
        acc[...] = total
        return carry

    lax.fori_loop(0, 9, tap, 0)

    for k in q_copies:
        k.wait_recv()
    half_a, half_b = pl.ds(0, 288), pl.ds(288, 288)
    a0, a1, b0, b1 = (pl.ds(q * ROWS, ROWS) for q in range(4))
    first = []
    for ref, slot, dev in (
        (kf.at[x, y, half_a], 30, xnext), (kf.at[x, y, half_a], 31, xprev),
        (kf.at[x, y, half_b], 32, ynext), (kf.at[x, y, half_b], 33, yprev),
    ):
        first.append(go(ref, ref, slot, dev))

    ge[...] = jax.nn.gelu(acc[...])
    for z in range(4):
        for k in range(16):
            here = (k // 4) * 16 + z * 4 + k % 4
            pieces[z, k] = ge[pl.ds(here, 8, stride=64), :].astype(BF16)
    qe[zl] = pieces[zl]
    p_copies = []
    for d in range(1, 4):
        there, dev = zpeer(d)
        p_copies.append(go(pieces.at[there], qe.at[zl], 48 + d, dev))

    for k in first:
        k.wait_recv()
    relay = []
    for ref, slot, dev in (
        (kf.at[xb, y, a0], 34, xnext), (kf.at[xa, y, a1], 35, xprev),
        (kf.at[x, yb, b0], 36, ynext), (kf.at[x, ya, b1], 37, yprev),
    ):
        relay.append(go(ref, ref, slot, dev))

    for k in p_copies:
        k.wait_recv()

    def p_copy(d):
        there, dev = ppeer(d)
        return pcp(qe.at[:, there], ph.at[m, x, :, y], 4, d, dev)

    plane(p_copy, begin)
    for z in range(4):
        ph[m, x, z, y] = qe[z, p]

    for k in relay:
        k.wait_recv()
    second = []
    for ref, slot, dev in (
        (kf.at[:, y, half_a], 38, ynext), (kf.at[:, y, half_a], 39, yprev),
        (kf.at[x, :, half_b], 40, xnext), (kf.at[x, :, half_b], 41, xprev),
    ):
        second.append(go(ref, ref, slot, dev))

    plane(p_copy, arrive)
    t_opp = go(ph.at[m], ph.at[m], 28, opp)
    t_sib = go(ph.at[m], ph.at[m], 29, sib)

    for k in second:
        k.wait_recv()
    last = []
    for ref, slot, dev in (
        (kf.at[:, yb, a0], 42, ynext), (kf.at[:, ya, a1], 43, yprev),
        (kf.at[xb, :, b0], 44, xnext), (kf.at[xa, :, b1], 45, xprev),
    ):
        last.append(go(ref, ref, slot, dev))

    t_opp.wait_recv()
    t_fwd = go(ph.at[m2], ph.at[m2], 26, sib)
    plane(x_copy, arrive)
    plane(g_copy, arrive)
    t_sib.wait_recv()
    t_fwd.wait_recv()

    extra = ex[...].reshape(512, 128)
    wide_extra = extra.astype(F32)
    masked = wide_extra[:, 8:9]
    e_parts = [(ph[b].reshape(512, 128).astype(F32) * (1.0 - masked)).astype(BF16) for b in range(4)]
    e = jnp.concatenate(e_parts + [extra], axis=1)
    g_all = gl[...]
    g_scaled = jnp.concatenate([g_all[0:512], 2.0 * g_all[512:528], jnp.zeros((112, 128), F32)], axis=0)
    g_high = g_scaled.astype(BF16)
    g_low = (g_scaled - g_high.astype(F32)).astype(BF16)
    products = jnp.dot(e, jnp.concatenate([g_high, g_low], axis=1), preferred_element_type=F32)
    mine = (products[:, 0:128] + products[:, 128:256]) * (ph[m].reshape(512, 128).astype(F32) * (1.0 - masked))
    nb[0] = lax.dot_general(
        jnp.ones((8, 128), F32), mine, NT, precision=lax.Precision.HIGHEST, preferred_element_type=F32)
    n_opp = go(nb.at[0], nb.at[1], 46, opp)
    n_opp.wait_recv()
    nb[2] = nb[0] + nb[1]
    n_sib = go(nb.at[2], nb.at[3], 47, sib)
    n_sib.wait_recv()
    squares = jnp.transpose(nb[2] + nb[3])[:, 0:1]
    squares = squares + jnp.sum(wide_extra * (base0 + masked * base1), axis=1, keepdims=True)
    scale = lax.rsqrt(jnp.maximum(squares, 0.0) * (1.0 / 5120.0) + 1e-05)

    for k in last:
        k.wait_recv()
    pad = jnp.zeros((64, 256), BF16)
    for j in range(7):
        rhs = jnp.concatenate(
            [kf[(2 * j) // 4, (2 * j) % 4], kf[(2 * j + 1) // 4, (2 * j + 1) % 4]], axis=1)
        rhs = jnp.concatenate([rhs, pad], axis=0)
        qkv[:, j * 256:j * 256 + 256] = (jnp.dot(e, rhs, preferred_element_type=F32) * scale).astype(BF16)

    row = lax.broadcasted_iota(jnp.int32, (640, 128), 0) % 128
    col = lax.broadcasted_iota(jnp.int32, (640, 128), 1)
    keep_mask = (row % 4 == col % 4) & (row // 64 == col // 64) & (col <= row)

    def group(i, carry):
        rows = pl.ds(pl.multiple_of(i * 128, 128), 128)
        for h in range(2):
            q = jnp.concatenate(
                [qkv[rows, (h * 5 + g) * 128:(h * 5 + g) * 128 + 128] for g in range(5)], axis=0)
            k = qkv[rows, 1280 + h * 128:1408 + h * 128]
            v = qkv[rows, 1536 + h * 128:1664 + h * 128]
            s = lax.dot_general(q, k, NT, preferred_element_type=F32) * (1.0 / HEAD**0.5)
            s = jnp.where(keep_mask, s, -1e30)
            top = jnp.max(s, axis=1, keepdims=True)
            exps = jnp.exp(s - top)
            share = (exps / jnp.sum(exps, axis=1, keepdims=True)).astype(BF16)
            mixed = jnp.dot(share, v, preferred_element_type=F32).astype(BF16)
            for g in range(5):
                out[rows, (h * 5 + g) * 128:(h * 5 + g) * 128 + 128] = mixed[g * 128:g * 128 + 128]
        return carry

    lax.fori_loop(0, 4, group, 0)

    for k in started:
        k.wait_send()
    for make in (w_copy, e_copy, x_copy, g_copy, p_copy):
        plane(make, lambda k: k.wait_send())


VMEM = pl.BlockSpec(memory_space=pltpu.VMEM)
ANY = pl.BlockSpec(memory_space=pl.ANY)


def shards(
    frames_in, conv_weight, embed_weight, action_table, mask_embed, norm_gain,
    q_weight, k_weight, v_weight, action_ids, token_mask,
):
    attended = pl.pallas_call(
        whole_kernel,
        out_shape=jax.ShapeDtypeStruct((512, 1280), BF16),
        in_specs=[pl.BlockSpec(memory_space=pltpu.SMEM)] + [ANY] * 10,
        out_specs=VMEM,
        scratch_shapes=[
            pltpu.VMEM((2, 256, 128), BF16),
            pltpu.VMEM((8, 5120), F32),
            pltpu.VMEM((1, 5120), F32),
            pltpu.VMEM((1, 5120), F32),
            pltpu.VMEM((80, 1280), BF16),
            pltpu.VMEM((80, 256), BF16),
            pltpu.VMEM((80, 256), BF16),
            pltpu.VMEM((2, 256), jnp.int32),
            pltpu.VMEM((WIN, 128), F32),
            pltpu.VMEM((27, 512, 128), BF16),
            pltpu.VMEM((4, 4, 256, 128), BF16),
            pltpu.VMEM((3, 4, 18, 16, 512), BF16),
            pltpu.VMEM((512, 128), F32),
            pltpu.VMEM((512, 128), F32),
            pltpu.VMEM((4, 16, 8, 128), BF16),
            pltpu.VMEM((4, 16, 8, 128), BF16),
            pltpu.VMEM((4, 16, 8, 128), BF16),
            pltpu.VMEM((4, 16, 8, 128), BF16),
            pltpu.VMEM((4, 4, 4, 8, 128), BF16),
            pltpu.VMEM((4, 4, 4, 4, 8, 128), BF16),
            pltpu.VMEM((16, 80, 128), BF16),
            pltpu.VMEM((DEPTH, 128), BF16),
            pltpu.VMEM((64, 8, DEPTH), BF16),
            pltpu.VMEM((32, DEPTH), BF16),
            pltpu.VMEM((48, 128), F32),
            pltpu.VMEM((4, 48, 128), F32),
            pltpu.VMEM((528, 128), F32),
            pltpu.VMEM((576, 128), BF16),
            pltpu.VMEM((4, ROWS, 128), BF16),
            pltpu.VMEM((4, 4, 576, 128), BF16),
            pltpu.VMEM((4, 8, 512), F32),
            pltpu.VMEM((512, 1792), BF16),
            pltpu.SemaphoreType.DMA((13,)),
            pltpu.SemaphoreType.DMA((52,)),
            pltpu.SemaphoreType.DMA((52,)),
            pltpu.SemaphoreType.DMA((5, 16)),
            pltpu.SemaphoreType.DMA((5, 16)),
        ],
        compiler_params=pltpu.CompilerParams(
            collective_id=0, has_side_effects=True, vmem_limit_bytes=60 * 1024 * 1024
        ),
        name="whole",
    )(
        action_ids, frames_in.reshape(2, 256, 128), conv_weight, embed_weight.reshape(16, 8, 5120),
        action_table, mask_embed.reshape(1, 5120), norm_gain.reshape(1, 5120), q_weight, k_weight, v_weight, token_mask,
    )
    return attended.reshape(128, 4, 1, 1280)


def solution(mesh):
    return jax.shard_map(
        shards,
        mesh=mesh,
        in_specs=(
            P("wide", None, None, "narrow"),
            P(None, None, "narrow"),
            P("narrow", None),
            P(),
            P(),
            P(),
            P("wide", "narrow"),
            P("wide", "narrow"),
            P("wide", "narrow"),
            P("wide"),
            P("wide", None),
        ),
        out_specs=P(None, None, "wide", "narrow"),
        check_vma=False,
    )
```

```python
import jax
import jax.numpy as jnp
from jax import lax
from jax.experimental import pallas as pl
from jax.experimental.pallas import tpu as pltpu
from jax.sharding import PartitionSpec as P

MESH = pl.DeviceIdType.MESH
F32 = jnp.float32
BF16 = jnp.bfloat16
HEAD = 128
WIN = 384
DEPTH = 4 * WIN
NT = (((1,), (1,)), ((), ()))


def whole_kernel(
    ids, fr_hbm, cw_hbm, ew_hbm, at_hbm, me_hbm, ga_hbm, qw_hbm, kw_hbm, vw_hbm, tm_hbm,
    out,
    fr, at, me, ga, qw, kw, vw, tm, gc, cw, xr, sh, acc, ge, pieces, qe, xx, qx, ex, ph, ws, wb, fb, sb, gp, gr, gl, ka, kr, kf, nb, sc, qkv,
    lsem, ssem, rsem, psend, precv,
):
    w = lax.axis_index("wide")
    n = lax.axis_index("narrow")
    x, zl, y = w // 16, (w // 4) % 4, w % 4
    zh, c = n // 2, n % 2
    p = x * 4 + y
    n1, n2 = zh * 2 + (1 - c), (1 - zh) * 2 + c
    m, m1, m2 = c * 2 + zh, (1 - c) * 2 + zh, c * 2 + (1 - zh)
    odd = zl % 2
    start = (zl * 320 // 128) * 128

    def at_plane(px, py):
        return px * 16 + zl * 4 + py

    def zpeer(d):
        z = (zl + d) % 4
        return z, (x * 16 + z * 4 + y, n)

    def ppeer(d):
        px, py = (x + d // 4) % 4, (y + d % 4) % 4
        return px * 4 + py, (at_plane(px, py), n)

    sib, opp = (w, n1), (w, n2)
    wnext, wprev = ((w + 1) % 64, n), ((w + 63) % 64, n)
    xa, xb = (x + 1) % 4, (x + 3) % 4
    ya, yb = (y + 1) % 4, (y + 3) % 4
    xnext, xprev = (at_plane(xa, y), n), (at_plane(xb, y), n)
    ynext, yprev = (at_plane(x, ya), n), (at_plane(x, yb), n)

    def cp(src, dst, slot, dev):
        return pltpu.make_async_remote_copy(
            src_ref=src, dst_ref=dst, send_sem=ssem.at[slot], recv_sem=rsem.at[slot],
            device_id=dev, device_id_type=MESH,
        )

    started = []

    def go(src, dst, slot, dev):
        k = cp(src, dst, slot, dev)
        k.start()
        started.append(k)
        return k

    def pcp(src, dst, group, d, dev):
        return pltpu.make_async_remote_copy(
            src_ref=src, dst_ref=dst, send_sem=psend.at[group], recv_sem=precv.at[group],
            device_id=dev, device_id_type=MESH,
        )

    def plane(make, op):
        def body(d, carry):
            op(make(d))
            return carry
        lax.fori_loop(1, 16, body, 0)

    def begin(k):
        k.start()

    def whole_group(group):
        ref = (wb.at[pl.ds(0, 1200)], fb.at[pl.ds(0, 15)], pieces.at[:, pl.ds(0, 15)], gl.at[pl.ds(0, 480)],
               pieces.at[:, pl.ds(0, 15)])[group]
        return pcp(ref, ref, group, 1, ppeer(1)[1])

    e_loads = []
    for i in range(4):
        e_loads.append(pltpu.make_async_copy(
            ew_hbm.at[:, :, pl.ds(pl.multiple_of(1280 * i + start, 128), WIN)],
            fb.at[pl.ds(m * 16, 16), :, pl.ds(WIN * i, WIN)],
            lsem.at[i],
        ))
        e_loads[-1].start()
    loads = []
    for i, (src, dst) in enumerate((
        (fr_hbm, fr), (ga_hbm, ga), (qw_hbm, qw), (kw_hbm, kw), (vw_hbm, vw), (at_hbm, at), (me_hbm, me), (tm_hbm, tm),
        (cw_hbm, cw),
    )):
        loads.append(pltpu.make_async_copy(src, dst, lsem.at[4 + i]))
        loads[-1].start()
    taps = loads.pop()

    barrier = pltpu.get_barrier_semaphore()

    def greet(dev):
        pl.semaphore_signal(barrier, inc=1, device_id=dev, device_id_type=MESH)

    for dev in (sib, opp, wnext, wprev, zpeer(1)[1], zpeer(2)[1], zpeer(3)[1]):
        greet(dev)

    def greet_plane(d, carry):
        greet(ppeer(d)[1])
        return carry

    lax.fori_loop(1, 16, greet_plane, 0)

    for i in range(4):
        wb[pl.ds(pl.multiple_of(i * WIN + (1 - odd) * 320, 16), 64), :] = jnp.zeros((64, 128), BF16)
    zero_row = jnp.zeros((4, 1, 16, 512), BF16)
    for dw in range(3):
        sh[dw, :, 0:1] = zero_row
        sh[dw, :, 17:18] = zero_row

    def w_rows(px, py):
        return pl.ds(pl.multiple_of(px * WIN + odd * 64 + py * 80, 16), 80)

    for k in e_loads + loads:
        k.wait()
    pl.semaphore_wait(barrier, 22)

    e_opp = go(fb.at[m * 16 + p], fb.at[m * 16 + p], 11, opp)
    f_opp = go(fr, xr.at[n, pl.ds(1, 2)], 1, opp)
    h_next = go(fr.at[1], xr.at[n, 0], 3, wnext)
    h_prev = go(fr.at[0], xr.at[n, 3], 4, wprev)
    f_sib = go(fr, xr.at[n, pl.ds(1, 2)], 0, sib)
    e_sib = go(fb.at[pl.ds(m * 16, 16)], fb.at[pl.ds(m * 16, 16)], 12, sib)

    cols = pl.ds(pl.multiple_of(1280 * x + start, 128), WIN)
    gain = jnp.broadcast_to(ga[:, cols], (8, WIN))
    for i in range(3):
        gc[i * 128:i * 128 + 128] = jnp.transpose(
            jnp.concatenate([gain[:, i * 128:i * 128 + 128], jnp.zeros((120, 128), F32)], axis=0))
    gain = gc[pl.ds(pl.multiple_of(odd * 64 + y * 80, 8), 80), :][:, 0:1]
    for t in range(14):
        source, col = (qw, t) if t < 10 else ((kw, t - 10) if t < 12 else (vw, t - 12))
        ws[t] = (source[:, col * 128:col * 128 + 128].astype(F32) * gain).astype(BF16)
    for t in range(14, 16):
        ws[t] = jnp.zeros((80, 128), BF16)

    def w_copy(d):
        there, dev = ppeer(d)
        return pcp(ws.at[there], wb.at[w_rows(x, y)], 0, d, dev)

    plane(w_copy, begin)
    wb[w_rows(x, y), :] = ws[p]
    xr[n, 1:3] = fr[...]

    e_opp.wait_recv()

    def e_copy(d):
        there, dev = ppeer(d)
        return pcp(fb.at[m2 * 16 + p], fb.at[m2 * 16 + p], 1, d, dev)

    plane(e_copy, begin)

    lane = lax.broadcasted_iota(jnp.int32, (4, 128), 1)
    onehot = jnp.concatenate([jnp.where(lane == ids[f], 1.0, 0.0) for f in range(2)], axis=0)
    lane8 = jnp.where(lax.broadcasted_iota(jnp.int32, (8, 128), 1) == 8, 1.0, 0.0)
    masks = jnp.concatenate(
        [tm[f:f + 1, i * 64:i * 64 + 64] for f in range(2) for i in range(4)], axis=0)
    masks = jnp.where(masks == 1, 1.0, 0.0)
    for z in range(4):
        for k in range(16):
            where = (k // 4) * 16 + z * 4 + k % 4
            xx[z, k] = (onehot + masks[:, where:where + 1] * lane8).astype(BF16)
    qx[zl] = xx[zl]
    x_copies = []
    for d in range(1, 4):
        there, dev = zpeer(d)
        x_copies.append(go(xx.at[there], qx.at[zl], 12 + d, dev))

    for i in range(4):
        cols = pl.ds(pl.multiple_of(1280 * i + start, 128), WIN)
        rows = jnp.concatenate([at[:, cols], me[:, cols], jnp.zeros((7, WIN), F32)], axis=0)
        high = rows.astype(BF16)
        sb[0:16, i * WIN:i * WIN + WIN] = high
        sb[16:32, i * WIN:i * WIN + WIN] = (rows - high.astype(F32)).astype(BF16)

    f_opp.wait_recv()
    h2_next = go(xr.at[n2, 2], xr.at[n2, 0], 5, wnext)
    h2_prev = go(xr.at[n2, 1], xr.at[n2, 3], 6, wprev)
    f_fwd = go(xr.at[n2, pl.ds(1, 2)], xr.at[n2, pl.ds(1, 2)], 2, sib)
    h_next.wait_recv()
    h_prev.wait_recv()
    s_copies = [go(xr.at[n, 0], xr.at[n, 0], 7, sib), go(xr.at[n, 3], xr.at[n, 3], 8, sib)]

    whole_group(1).wait_recv()
    e_fwd = go(fb.at[pl.ds(m2 * 16, 16)], fb.at[pl.ds(m2 * 16, 16)], 10, sib)
    for k in x_copies:
        k.wait_recv()

    def x_copy(d):
        there, dev = ppeer(d)
        return pcp(qx.at[:, there], ex.at[x, :, y], 2, d, dev)

    plane(x_copy, begin)
    for z in range(4):
        ex[x, z, y] = qx[z, p]

    column = lax.broadcasted_iota(jnp.int32, (256, 128), 0) % 16

    def shift(slot, carry):
        edge = ((w == 0) & (slot == 0)) | ((w == 63) & (slot == 3))
        keep = jnp.where(edge, 0.0, 1.0)
        for b in range(4):
            cells = xr[b, slot].astype(F32) * keep
            lanes = slice(b * 128, b * 128 + 128)
            left = jnp.where(column == 0, 0.0, pltpu.roll(cells, 1, 0))
            right = jnp.where(column == 15, 0.0, pltpu.roll(cells, 255, 0))
            for dw, part in enumerate((left, cells, right)):
                sh[dw, slot, 1:17, :, lanes] = part.astype(BF16).reshape(16, 16, 128)
        return carry

    def taps_of(dt):
        def tap(dh, carry):
            total = acc[...]
            for dw in range(3):
                lhs = sh[dw, dt:dt + 2, pl.ds(dh, 16)].reshape(512, 512)
                total = total + jnp.dot(lhs, cw[dt * 9 + dh * 3 + dw], preferred_element_type=F32)
            acc[...] = total
            return carry
        lax.fori_loop(0, 3, tap, 0)

    f_sib.wait_recv()
    f_fwd.wait_recv()
    lax.fori_loop(1, 3, shift, 0)

    h2_next.wait_recv()
    h2_prev.wait_recv()
    s_copies += [go(xr.at[n2, 0], xr.at[n2, 0], 9, sib), go(xr.at[n2, 3], xr.at[n2, 3], 25, sib)]

    whole_group(0).wait_recv()
    e_sib.wait_recv()
    e_fwd.wait_recv()

    for b in range(4):
        part = jnp.dot(fb[b * 16:b * 16 + 16].reshape(128, DEPTH), wb[...], preferred_element_type=F32)
        ka[b, 0:128] = part.astype(BF16)
    both = jnp.dot(sb[...], wb[...], preferred_element_type=F32)
    for b in range(4):
        ka[b, 128:144] = (both[0:16] + both[16:32]).astype(BF16)
    k_copies = []
    for d in range(1, 4):
        there, dev = zpeer(d)
        k_copies.append(go(ka.at[there], kr.at[zl], 18 + d, dev))
    kr[zl] = ka[zl]

    where = lax.broadcasted_iota(jnp.int32, (128, DEPTH), 1) % WIN
    valid = jnp.where(odd == 1, jnp.where(where >= 64, 1.0, 0.0), jnp.where(where < 320, 1.0, 0.0))
    block = (fb[pl.ds(m * 16, 16)].reshape(128, DEPTH).astype(F32) * valid).astype(BF16)
    gp[0:32] = lax.dot_general(
        fb[pl.ds(p * 4, 4)].reshape(32, DEPTH), block, NT, preferred_element_type=F32)
    both = lax.dot_general(sb[...], block, NT, preferred_element_type=F32)
    gp[32:48] = both[0:16] + both[16:32]
    g_copies = []
    for d in range(1, 4):
        there, dev = zpeer(d)
        g_copies.append(go(gp, gr.at[zl], 15 + d, dev))
    gr[zl] = gp[...]

    taps.wait()
    acc[...] = jnp.zeros(acc.shape, F32)
    taps_of(1)

    for k in k_copies:
        k.wait_recv()
    ksum = (kr[0].astype(F32) + kr[1].astype(F32)) + (kr[2].astype(F32) + kr[3].astype(F32))

    def quarter():
        return pl.ds(pl.multiple_of(zl * 128, 16), 128)

    kf[x, y, quarter(), :] = ksum[0:128].astype(BF16)
    kf[x, y, 512:528, :] = ksum[128:144].astype(BF16)
    q_copies = []
    for d in range(1, 4):
        there, dev = zpeer(d)
        q_copies.append(go(kf.at[x, y, quarter()], kf.at[x, y, quarter()], 21 + d, dev))

    for k in s_copies:
        k.wait_recv()
    lax.fori_loop(0, 2, lambda i, carry: shift(i * 3, carry), 0)

    taps_of(0)

    taps_of(2)

    ge[...] = jax.nn.gelu(acc[...])
    for z in range(4):
        for k in range(16):
            here = (k // 4) * 16 + z * 4 + k % 4
            pieces[z, k] = ge[pl.ds(here, 8, stride=64), :].astype(BF16)
    p_copies = []
    for d in range(1, 4):
        there, dev = zpeer(d)
        p_copies.append(go(pieces.at[there], qe.at[zl], 25 + d, dev))
    qe[zl] = pieces[zl]

    for k in g_copies:
        k.wait_recv()
    gsum = (gr[0] + gr[1]) + (gr[2] + gr[3])

    def g_rows():
        return pl.ds(pl.multiple_of(p * 32, 8), 32)

    gl[g_rows(), :] = gsum[0:32]
    gl[512:528] = gsum[32:48]

    half_a, half_b = pl.ds(0, 256), pl.ds(256, 272)
    a0, a1, b0, b1 = pl.ds(0, 128), pl.ds(128, 128), pl.ds(256, 144), pl.ds(400, 128)
    xc, yc = (x + 2) % 4, (y + 2) % 4

    def tile(tx, ty, rows, slot, dev):
        return go(kf.at[tx, ty, rows], kf.at[tx, ty, rows], 30 + slot, dev)

    for k in q_copies:
        k.wait_recv()
    near = [
        tile(x, y, half_a, 0, xnext), tile(x, y, half_a, 1, xprev),
        tile(x, y, half_b, 2, ynext), tile(x, y, half_b, 3, yprev),
    ]
    own = [
        tile(x, y, half_a, 4, ynext), tile(x, y, half_a, 5, yprev),
        tile(x, y, half_b, 6, xnext), tile(x, y, half_b, 7, xprev),
    ]

    for k in near:
        k.wait_recv()
    far = [
        tile(xb, y, a0, 8, xnext), tile(xa, y, a1, 9, xprev),
        tile(x, yb, b0, 10, ynext), tile(x, ya, b1, 11, yprev),
    ]
    def g_copy(d):
        there, dev = ppeer(d)
        return pcp(gl.at[g_rows()], gl.at[g_rows()], 3, d, dev)

    plane(g_copy, begin)

    for k in p_copies:
        k.wait_recv()

    def p_copy(d):
        there, dev = ppeer(d)
        return pcp(qe.at[:, there], ph.at[m, x, :, y], 4, d, dev)

    plane(p_copy, begin)
    for z in range(4):
        ph[m, x, z, y] = qe[z, p]

    turned = []
    for i, (tx, ty) in enumerate(((xb, yb), (xa, ya))):
        turned += [
            tile(tx, y, half_a, 12 + 4 * i, ynext), tile(tx, y, half_a, 13 + 4 * i, yprev),
            tile(x, ty, half_b, 14 + 4 * i, xnext), tile(x, ty, half_b, 15 + 4 * i, xprev),
        ]

    whole_group(4).wait_recv()
    t_opp = go(ph.at[m], ph.at[m], 29, opp)
    t_sib = go(ph.at[m], ph.at[m], 70, sib)

    for k in own:
        k.wait_recv()
    ends = [
        tile(x, yb, a0, 20, ynext), tile(x, ya, a1, 21, yprev),
        tile(xb, y, b0, 22, xnext), tile(xa, y, b1, 23, xprev),
    ]
    for k in far:
        k.wait_recv()
    across = [
        tile(xc, y, half_a, 24, ynext), tile(xc, y, half_a, 25, yprev),
        tile(x, yc, half_b, 26, xnext), tile(x, yc, half_b, 27, xprev),
    ]

    for k in turned:
        k.wait_recv()
    ends += [
        tile(xb, yb, a0, 28, ynext), tile(xb, ya, a1, 29, yprev),
        tile(xa, yb, a0, 30, ynext), tile(xa, ya, a1, 31, yprev),
        tile(xb, yb, b0, 32, xnext), tile(xa, yb, b1, 33, xprev),
        tile(xb, ya, b0, 34, xnext), tile(xa, ya, b1, 35, xprev),
    ]

    for k in across:
        k.wait_recv()
    ends += [
        tile(xc, yb, a0, 36, ynext), tile(xc, ya, a1, 37, yprev),
        tile(xb, yc, b0, 38, xnext), tile(xa, yc, b1, 39, xprev),
    ]

    table = at[...]
    masked_row = me[...]
    squares0 = jnp.sum(table * table, axis=1, keepdims=True)
    squares1 = 2.0 * jnp.sum(table * masked_row, axis=1, keepdims=True) + jnp.sum(masked_row * masked_row)
    empty = jnp.zeros((120, 128), F32)
    base0 = jnp.transpose(jnp.concatenate([jnp.broadcast_to(squares0, (8, 128)), empty], axis=0))[0:1, :]
    base1 = jnp.transpose(jnp.concatenate([jnp.broadcast_to(squares1, (8, 128)), empty], axis=0))[0:1, :]

    t_opp.wait_recv()
    t_fwd = go(ph.at[m2], ph.at[m2], 71, sib)
    whole_group(2).wait_recv()
    whole_group(3).wait_recv()
    t_sib.wait_recv()
    t_fwd.wait_recv()

    extra = ex[...].reshape(512, 128)
    wide_extra = extra.astype(F32)
    masked = wide_extra[:, 8:9]
    e_parts = [(ph[b].reshape(512, 128).astype(F32) * (1.0 - masked)).astype(BF16) for b in range(4)]
    e = jnp.concatenate(e_parts + [extra], axis=1)
    g_all = gl[...]
    g_scaled = jnp.concatenate([g_all[0:512], 2.0 * g_all[512:528], jnp.zeros((112, 128), F32)], axis=0)
    g_high = g_scaled.astype(BF16)
    g_low = (g_scaled - g_high.astype(F32)).astype(BF16)
    products = jnp.dot(e, jnp.concatenate([g_high, g_low], axis=1), preferred_element_type=F32)
    mine = (products[:, 0:128] + products[:, 128:256]) * (ph[m].reshape(512, 128).astype(F32) * (1.0 - masked))
    nb[0] = lax.dot_general(
        jnp.ones((8, 128), F32), mine, NT, precision=lax.Precision.HIGHEST, preferred_element_type=F32)
    n_opp = go(nb.at[0], nb.at[1], 72, opp)
    own_base = jnp.concatenate([base0, base1, lane8[0:1], jnp.zeros((5, 128), F32)], axis=0)
    base = lax.dot_general(own_base, wide_extra, NT, precision=lax.Precision.HIGHEST, preferred_element_type=F32)
    base = base[0:1] + base[2:3] * base[1:2]

    for k in ends:
        k.wait_recv()
    pad = jnp.zeros((112, 256), BF16)

    def project(j):
        rhs = jnp.concatenate(
            [kf[(2 * j) // 4, (2 * j) % 4], kf[(2 * j + 1) // 4, (2 * j + 1) % 4]], axis=1)
        rhs = jnp.concatenate([rhs, pad], axis=0)
        qkv[:, j * 256:j * 256 + 256] = jnp.dot(e, rhs, preferred_element_type=F32).astype(BF16)

    for j in range(5):
        project(j)
    n_opp.wait_recv()
    nb[2] = nb[0] + nb[1]
    n_sib = go(nb.at[2], nb.at[3], 73, sib)
    for j in range(5, 7):
        project(j)
    n_sib.wait_recv()
    squares = nb[2] + nb[3] + base
    scale = lax.rsqrt(jnp.maximum(squares, 0.0) * (1.0 / 5120.0) + 1e-05)
    nb[4] = scale
    sc[...] = jnp.transpose(scale)

    row = lax.broadcasted_iota(jnp.int32, (640, 128), 0) % 128
    col = lax.broadcasted_iota(jnp.int32, (640, 128), 1)
    keep_mask = (row % 4 == col % 4) & (row // 64 == col // 64) & (col <= row)

    def group(i, carry):
        rows = pl.ds(pl.multiple_of(i * 128, 128), 128)
        col_scale = nb[4, 0:1, rows]
        row_scale = jnp.concatenate([sc[rows, 0:1] * (1.0 / HEAD**0.5)] * 5, axis=0)
        for h in range(2):
            q = jnp.concatenate(
                [qkv[rows, (h * 5 + g) * 128:(h * 5 + g) * 128 + 128] for g in range(5)], axis=0)
            k = qkv[rows, 1280 + h * 128:1408 + h * 128]
            v = qkv[rows, 1536 + h * 128:1664 + h * 128]
            s = lax.dot_general(q, k, NT, preferred_element_type=F32) * row_scale * col_scale
            s = jnp.where(keep_mask, s, -1e30)
            top = jnp.max(s, axis=1, keepdims=True)
            exps = jnp.exp(s - top)
            total = jnp.sum(exps, axis=1, keepdims=True)
            mixed = jnp.dot((exps * col_scale).astype(BF16), v, preferred_element_type=F32)
            mixed = (mixed / total).astype(BF16)
            for g in range(5):
                out[pl.ds(i * 32, 32), :, (h * 5 + g) * 128:(h * 5 + g) * 128 + 128] = mixed[g * 128:g * 128 + 128].reshape(32, 4, 128)
        return carry

    lax.fori_loop(0, 4, group, 0)

    for k in started:
        k.wait_send()
    for group in range(5):
        whole_group(group).wait_send()


VMEM = pl.BlockSpec(memory_space=pltpu.VMEM)
ANY = pl.BlockSpec(memory_space=pl.ANY)


def shards(
    frames_in, conv_weight, embed_weight, action_table, mask_embed, norm_gain,
    q_weight, k_weight, v_weight, action_ids, token_mask,
):
    attended = pl.pallas_call(
        whole_kernel,
        out_shape=jax.ShapeDtypeStruct((128, 4, 1280), BF16),
        in_specs=[pl.BlockSpec(memory_space=pltpu.SMEM)] + [ANY] * 10,
        out_specs=VMEM,
        scratch_shapes=[
            pltpu.VMEM((2, 256, 128), BF16),
            pltpu.VMEM((8, 5120), F32),
            pltpu.VMEM((1, 5120), F32),
            pltpu.VMEM((1, 5120), F32),
            pltpu.VMEM((80, 1280), BF16),
            pltpu.VMEM((80, 256), BF16),
            pltpu.VMEM((80, 256), BF16),
            pltpu.VMEM((2, 256), jnp.int32),
            pltpu.VMEM((WIN, 128), F32),
            pltpu.VMEM((27, 512, 128), BF16),
            pltpu.VMEM((4, 4, 256, 128), BF16),
            pltpu.VMEM((3, 4, 18, 16, 512), BF16),
            pltpu.VMEM((512, 128), F32),
            pltpu.VMEM((512, 128), F32),
            pltpu.VMEM((4, 16, 8, 128), BF16),
            pltpu.VMEM((4, 16, 8, 128), BF16),
            pltpu.VMEM((4, 16, 8, 128), BF16),
            pltpu.VMEM((4, 16, 8, 128), BF16),
            pltpu.VMEM((4, 4, 4, 8, 128), BF16),
            pltpu.VMEM((4, 4, 4, 4, 8, 128), BF16),
            pltpu.VMEM((16, 80, 128), BF16),
            pltpu.VMEM((DEPTH, 128), BF16),
            pltpu.VMEM((64, 8, DEPTH), BF16),
            pltpu.VMEM((32, DEPTH), BF16),
            pltpu.VMEM((48, 128), F32),
            pltpu.VMEM((4, 48, 128), F32),
            pltpu.VMEM((528, 128), F32),
            pltpu.VMEM((4, 144, 128), BF16),
            pltpu.VMEM((4, 144, 128), BF16),
            pltpu.VMEM((4, 4, 528, 128), BF16),
            pltpu.VMEM((5, 8, 512), F32),
            pltpu.VMEM((512, 8), F32),
            pltpu.VMEM((512, 1792), BF16),
            pltpu.SemaphoreType.DMA((13,)),
            pltpu.SemaphoreType.DMA((74,)),
            pltpu.SemaphoreType.DMA((74,)),
            pltpu.SemaphoreType.DMA((5,)),
            pltpu.SemaphoreType.DMA((5,)),
        ],
        compiler_params=pltpu.CompilerParams(
            collective_id=0, has_side_effects=True, vmem_limit_bytes=60 * 1024 * 1024
        ),
        name="whole",
    )(
        action_ids, frames_in.reshape(2, 256, 128), conv_weight, embed_weight.reshape(16, 8, 5120),
        action_table, mask_embed.reshape(1, 5120), norm_gain.reshape(1, 5120), q_weight, k_weight, v_weight, token_mask,
    )
    return attended.reshape(128, 4, 1, 1280)


def solution(mesh):
    return jax.shard_map(
        shards,
        mesh=mesh,
        in_specs=(
            P("wide", None, None, "narrow"),
            P(None, None, "narrow"),
            P("narrow", None),
            P(),
            P(),
            P(),
            P("wide", "narrow"),
            P("wide", "narrow"),
            P("wide", "narrow"),
            P("wide"),
            P("wide", None),
        ),
        out_specs=P(None, None, "wide", "narrow"),
        check_vma=False,
    )
```

```python
import jax
import jax.numpy as jnp
from jax import lax
from jax.experimental import pallas as pl
from jax.experimental.pallas import tpu as pltpu
from jax.sharding import PartitionSpec as P

MESH = pl.DeviceIdType.MESH
F32 = jnp.float32
BF16 = jnp.bfloat16
HEAD = 128
WIN = 384
DEPTH = 4 * WIN
NT = (((1,), (1,)), ((), ()))


def whole_kernel(
    ids, fr_hbm, cw_hbm, ew_hbm, at_hbm, me_hbm, ga_hbm, qw_hbm, kw_hbm, vw_hbm, tm_hbm,
    out,
    fr, at, me, ga, qw, kw, vw, tm, gc, cw, xr, acc, ge, pieces, qe, xx, qx, ex, ph, ws, wb, fb, sb, gp, gr, gl, ka, kr, kf, nb, sc, qkv,
    lsem, ssem, rsem, psend, precv,
):
    w = lax.axis_index("wide")
    n = lax.axis_index("narrow")
    x, zl, y = w // 16, (w // 4) % 4, w % 4
    zh, c = n // 2, n % 2
    p = x * 4 + y
    n1, n2, n3 = zh * 2 + (1 - c), (1 - zh) * 2 + c, (1 - zh) * 2 + (1 - c)
    m, m1, m2 = c * 2 + zh, (1 - c) * 2 + zh, c * 2 + (1 - zh)
    odd = zl % 2
    start = (zl * 320 // 128) * 128

    def at_plane(px, py):
        return px * 16 + zl * 4 + py

    xs, ys, zs = ([at] + [(at + d) % 4 for d in range(1, 4)] for at in (x, y, zl))

    def zpeer(d):
        return zs[d], (x * 16 + zs[d] * 4 + y, n)

    def ppeer(d):
        px, py = xs[d // 4], ys[d % 4]
        return px * 4 + py, (at_plane(px, py), n)

    sib, opp = (w, n1), (w, n2)
    wnext, wprev = ((w + 1) % 64, n), ((w + 63) % 64, n)
    xa, xc, xb = xs[1:]
    ya, yc, yb = ys[1:]
    xnext, xprev = (at_plane(xa, y), n), (at_plane(xb, y), n)
    ynext, yprev = (at_plane(x, ya), n), (at_plane(x, yb), n)

    def cp(src, dst, slot, dev):
        return pltpu.make_async_remote_copy(
            src_ref=src, dst_ref=dst, send_sem=ssem.at[slot], recv_sem=rsem.at[slot],
            device_id=dev, device_id_type=MESH,
        )

    started = []

    def go(src, dst, slot, dev):
        k = cp(src, dst, slot, dev)
        k.start()
        started.append(k)
        return k

    def pcp(src, dst, group, d, dev):
        return pltpu.make_async_remote_copy(
            src_ref=src, dst_ref=dst, send_sem=psend.at[group], recv_sem=precv.at[group],
            device_id=dev, device_id_type=MESH,
        )

    def plane(make, op):
        for d in range(1, 16):
            op(make(d))

    def begin(k):
        k.start()

    def whole_group(group):
        ref = (wb.at[pl.ds(0, 1200)], fb.at[pl.ds(0, 15)], pieces.at[:, pl.ds(0, 15)], gl.at[pl.ds(0, 480)],
               pieces.at[:, pl.ds(0, 15)])[group]
        return pcp(ref, ref, group, 1, ppeer(1)[1])

    e_loads = []
    for i in range(4):
        e_loads.append(pltpu.make_async_copy(
            ew_hbm.at[:, :, pl.ds(pl.multiple_of(1280 * i + start, 128), WIN)],
            fb.at[pl.ds(m * 16, 16), :, pl.ds(WIN * i, WIN)],
            lsem.at[i],
        ))
        e_loads[-1].start()
    loads = []
    for i, (src, dst) in enumerate((
        (fr_hbm, fr), (ga_hbm, ga), (qw_hbm, qw), (kw_hbm, kw), (vw_hbm, vw), (at_hbm, at), (me_hbm, me), (tm_hbm, tm),
        (cw_hbm, cw),
    )):
        loads.append(pltpu.make_async_copy(src, dst, lsem.at[4 + i]))
        loads[-1].start()
    taps = loads.pop()

    barrier = pltpu.get_barrier_semaphore()

    def greet(dev):
        pl.semaphore_signal(barrier, inc=1, device_id=dev, device_id_type=MESH)

    for dev in (sib, opp, (w, n3), wnext, wprev, zpeer(1)[1], zpeer(2)[1], zpeer(3)[1]):
        greet(dev)

    for d in range(1, 16):
        greet(ppeer(d)[1])

    for i in range(4):
        wb[pl.ds(pl.multiple_of(i * WIN + (1 - odd) * 320, 16), 64), :] = jnp.zeros((64, 128), BF16)
    zero_row = jnp.zeros((4, 4, 1, 16, 128), BF16)
    xr[:, :, 0:1] = zero_row
    xr[:, :, 17:18] = zero_row

    def w_rows(px, py):
        return pl.ds(pl.multiple_of(px * WIN + odd * 64 + py * 80, 16), 80)

    for k in e_loads + loads:
        k.wait()
    pl.semaphore_wait(barrier, 23)

    e_opp = go(fb.at[m * 16 + p], fb.at[m * 16 + p], 11, opp)
    inner = pl.ds(1, 16)
    f_opp = go(fr, xr.at[n, pl.ds(1, 2), inner], 1, opp)
    h_next = go(fr.at[1], xr.at[n, 0, inner], 3, wnext)
    h_prev = go(fr.at[0], xr.at[n, 3, inner], 4, wprev)
    f_sib = go(fr, xr.at[n, pl.ds(1, 2), inner], 0, sib)
    e_sib = go(fb.at[pl.ds(m * 16, 16)], fb.at[pl.ds(m * 16, 16)], 12, sib)

    cols = pl.ds(pl.multiple_of(1280 * x + start, 128), WIN)
    gain = jnp.broadcast_to(ga[:, cols], (8, WIN))
    for i in range(3):
        gc[i * 128:i * 128 + 128] = jnp.transpose(
            jnp.concatenate([gain[:, i * 128:i * 128 + 128], jnp.zeros((120, 128), F32)], axis=0))
    gain = gc[pl.ds(pl.multiple_of(odd * 64 + y * 80, 8), 80), :][:, 0:1]
    for t in range(14):
        source, col = (qw, t) if t < 10 else ((kw, t - 10) if t < 12 else (vw, t - 12))
        ws[t] = (source[:, col * 128:col * 128 + 128].astype(F32) * gain).astype(BF16)
    for t in range(14, 16):
        ws[t] = jnp.zeros((80, 128), BF16)

    def w_copy(d):
        there, dev = ppeer(d)
        return pcp(ws.at[there], wb.at[w_rows(x, y)], 0, d, dev)

    plane(w_copy, begin)
    wb[w_rows(x, y), :] = ws[p]
    xr[n, 1:3, 1:17] = fr[...]

    e_opp.wait_recv()

    def e_copy(d):
        there, dev = ppeer(d)
        return pcp(fb.at[m2 * 16 + p], fb.at[m2 * 16 + p], 1, d, dev)

    plane(e_copy, begin)

    lane = lax.broadcasted_iota(jnp.int32, (4, 128), 1)
    onehot = jnp.concatenate([jnp.where(lane == ids[f], 1.0, 0.0) for f in range(2)], axis=0)
    lane8 = jnp.where(lax.broadcasted_iota(jnp.int32, (8, 128), 1) == 8, 1.0, 0.0)
    masks = jnp.concatenate(
        [tm[f:f + 1, i * 64:i * 64 + 64] for f in range(2) for i in range(4)], axis=0)
    masks = jnp.where(masks == 1, 1.0, 0.0)
    for z in range(4):
        for k in range(16):
            where = (k // 4) * 16 + z * 4 + k % 4
            xx[z, k] = (onehot + masks[:, where:where + 1] * lane8).astype(BF16)
    qx[zl] = xx[zl]
    x_copies = []
    for d in range(1, 4):
        there, dev = zpeer(d)
        x_copies.append(go(xx.at[there], qx.at[zl], 12 + d, dev))

    for i in range(4):
        cols = pl.ds(pl.multiple_of(1280 * i + start, 128), WIN)
        rows = jnp.concatenate([at[:, cols], me[:, cols], jnp.zeros((7, WIN), F32)], axis=0)
        high = rows.astype(BF16)
        sb[0:16, i * WIN:i * WIN + WIN] = high
        sb[16:32, i * WIN:i * WIN + WIN] = (rows - high.astype(F32)).astype(BF16)

    f_opp.wait_recv()
    h2_next = go(xr.at[n2, 2, inner], xr.at[n2, 0, inner], 5, wnext)
    h2_prev = go(xr.at[n2, 1, inner], xr.at[n2, 3, inner], 6, wprev)
    f_fwd = go(xr.at[n2, pl.ds(1, 2), inner], xr.at[n2, pl.ds(1, 2), inner], 2, sib)
    h_next.wait_recv()
    h_prev.wait_recv()
    s_copies = [
        go(xr.at[n, 0, inner], xr.at[n, 0, inner], 7, sib), go(xr.at[n, 3, inner], xr.at[n, 3, inner], 8, sib)]

    whole_group(1).wait_recv()
    e_fwd = go(fb.at[pl.ds(m2 * 16, 16)], fb.at[pl.ds(m2 * 16, 16)], 10, sib)
    for k in x_copies:
        k.wait_recv()

    def x_copy(d):
        there, dev = ppeer(d)
        return pcp(qx.at[:, there], ex.at[x, :, y], 2, d, dev)

    plane(x_copy, begin)
    for z in range(4):
        ex[x, z, y] = qx[z, p]

    def taps_of(dt):
        def tap(dh, carry):
            total = acc[...]
            lhs = jnp.concatenate(
                [xr[b, dt:dt + 2, pl.ds(dh, 16)].reshape(512, 128) for b in range(4)], axis=1)
            rhs = jnp.concatenate([cw[dt * 9 + dh * 3 + dw] for dw in range(3)], axis=1)
            acc[...] = total + jnp.dot(lhs, rhs, preferred_element_type=F32)
            return carry
        lax.fori_loop(0, 3, tap, 0)

    f_sib.wait_recv()
    f_fwd.wait_recv()

    h2_next.wait_recv()
    h2_prev.wait_recv()
    s_copies += [
        go(xr.at[n2, 0, inner], xr.at[n2, 0, inner], 9, sib), go(xr.at[n2, 3, inner], xr.at[n2, 3, inner], 25, sib)]

    whole_group(0).wait_recv()
    e_sib.wait_recv()
    e_fwd.wait_recv()

    part = jnp.dot(fb[...].reshape(512, DEPTH), wb[...], preferred_element_type=F32)
    for b in range(4):
        ka[b, 0:128] = part[b * 128:b * 128 + 128].astype(BF16)
    both = jnp.dot(sb[...], wb[...], preferred_element_type=F32)
    for b in range(4):
        ka[b, 128:144] = (both[0:16] + both[16:32]).astype(BF16)
    k_copies = []
    for d in range(1, 4):
        there, dev = zpeer(d)
        k_copies.append(go(ka.at[there], kr.at[zl], 18 + d, dev))
    kr[zl] = ka[zl]

    where = lax.broadcasted_iota(jnp.int32, (1, WIN), 1) + (1 - odd) * 64
    valid = jnp.where(where >= 64, jnp.where(where < 384, 1.0, 0.0), 0.0)
    valid = jnp.concatenate([valid] * 4, axis=1)
    block = (fb[pl.ds(m * 16, 16)].reshape(128, DEPTH).astype(F32) * valid).astype(BF16)
    rows = jnp.concatenate([fb[pl.ds(p * 4, 4)].reshape(32, DEPTH), sb[...]], axis=0)
    both = lax.dot_general(rows, block, NT, preferred_element_type=F32)
    gp[0:32] = both[0:32]
    gp[32:48] = both[32:48] + both[48:64]
    g_copies = []
    for d in range(1, 4):
        there, dev = zpeer(d)
        g_copies.append(go(gp, gr.at[zl], 15 + d, dev))
    gr[zl] = gp[...]

    taps.wait()
    acc[...] = jnp.zeros(acc.shape, F32)
    taps_of(1)

    for k in k_copies:
        k.wait_recv()
    ksum = (kr[0].astype(F32) + kr[1].astype(F32)) + (kr[2].astype(F32) + kr[3].astype(F32))

    def quarter():
        return pl.ds(pl.multiple_of(zl * 128, 16), 128)

    kf[x, y, quarter(), :] = ksum[0:128].astype(BF16)
    kf[x, y, 512:528, :] = ksum[128:144].astype(BF16)
    q_copies = []
    for d in range(1, 4):
        there, dev = zpeer(d)
        q_copies.append(go(kf.at[x, y, quarter()], kf.at[x, y, quarter()], 21 + d, dev))

    for k in g_copies:
        k.wait_recv()
    gsum = (gr[0] + gr[1]) + (gr[2] + gr[3])

    def g_rows():
        return pl.ds(pl.multiple_of(p * 32, 8), 32)

    gl[g_rows(), :] = gsum[0:32]
    gl[512:528] = gsum[32:48]

    def g_copy(d):
        there, dev = ppeer(d)
        return pcp(gl.at[g_rows()], gl.at[g_rows()], 3, d, dev)

    plane(g_copy, begin)

    for k in s_copies:
        k.wait_recv()
    for k in s_copies:
        k.wait_send()
        started[:] = [other for other in started if other is not k]

    @pl.when(w == 0)
    def _():
        xr[:, 0, 1:17] = jnp.zeros((4, 16, 16, 128), BF16)

    @pl.when(w == 63)
    def _():
        xr[:, 3, 1:17] = jnp.zeros((4, 16, 16, 128), BF16)

    taps_of(0)

    taps_of(2)

    half_a, half_b = pl.ds(0, 256), pl.ds(256, 272)
    a0, a1, b0, b1 = pl.ds(0, 128), pl.ds(128, 128), pl.ds(256, 144), pl.ds(400, 128)

    def tile(tx, ty, rows, slot, dev):
        return go(kf.at[tx, ty, rows], kf.at[tx, ty, rows], 30 + slot, dev)

    for k in q_copies:
        k.wait_recv()
    near = [
        tile(x, y, half_a, 0, xnext), tile(x, y, half_a, 1, xprev),
        tile(x, y, half_b, 2, ynext), tile(x, y, half_b, 3, yprev),
    ]
    column = lax.broadcasted_iota(jnp.int32, (512, 128), 0) & 15
    left = jnp.where(column == 0, 0.0, pltpu.roll(acc[:, 0:128], 1, 0))
    right = jnp.where(column == 15, 0.0, pltpu.roll(acc[:, 256:384], 511, 0))
    ge[...] = jax.nn.gelu(acc[:, 128:256] + left + right)
    for z in range(4):
        for k in range(16):
            here = (k // 4) * 16 + z * 4 + k % 4
            pieces[z, k] = ge[pl.ds(here, 8, stride=64), :].astype(BF16)
    p_copies = []
    for d in range(1, 4):
        there, dev = zpeer(d)
        p_copies.append(go(pieces.at[there], qe.at[zl], 25 + d, dev))
    qe[zl] = pieces[zl]

    for k in near:
        k.wait_recv()
    far = [
        tile(xb, y, a0, 8, xnext), tile(xa, y, a1, 9, xprev),
        tile(x, yb, b0, 10, ynext), tile(x, ya, b1, 11, yprev),
    ]
    for k in p_copies:
        k.wait_recv()

    def p_copy(d):
        there, dev = ppeer(d)
        return pcp(qe.at[:, there], ph.at[m, x, :, y], 4, d, dev)

    plane(p_copy, begin)
    for z in range(4):
        ph[m, x, z, y] = qe[z, p]

    own = [
        tile(x, y, half_a, 4, ynext), tile(x, y, half_a, 5, yprev),
        tile(x, y, half_b, 6, xnext), tile(x, y, half_b, 7, xprev),
    ]

    turned = []
    for i, (tx, ty) in enumerate(((xb, yb), (xa, ya))):
        turned += [
            tile(tx, y, half_a, 12 + 4 * i, ynext), tile(tx, y, half_a, 13 + 4 * i, yprev),
            tile(x, ty, half_b, 14 + 4 * i, xnext), tile(x, ty, half_b, 15 + 4 * i, xprev),
        ]

    whole_group(4).wait_recv()
    t_opp = go(ph.at[m], ph.at[m], 29, opp)
    t_sib = go(ph.at[m], ph.at[m], 70, sib)

    for k in own:
        k.wait_recv()
    ends = [
        tile(x, yb, a0, 20, ynext), tile(x, ya, a1, 21, yprev),
        tile(xb, y, b0, 22, xnext), tile(xa, y, b1, 23, xprev),
    ]
    for k in far:
        k.wait_recv()
    across = [
        tile(xc, y, half_a, 24, ynext), tile(xc, y, half_a, 25, yprev),
        tile(x, yc, half_b, 26, xnext), tile(x, yc, half_b, 27, xprev),
    ]

    for k in turned:
        k.wait_recv()
    ends += [
        tile(xb, yb, a0, 28, ynext), tile(xb, ya, a1, 29, yprev),
        tile(xa, yb, a0, 30, ynext), tile(xa, ya, a1, 31, yprev),
        tile(xb, yb, b0, 32, xnext), tile(xa, yb, b1, 33, xprev),
        tile(xb, ya, b0, 34, xnext), tile(xa, ya, b1, 35, xprev),
    ]

    for k in across:
        k.wait_recv()
    ends += [
        tile(xc, yb, a0, 36, ynext), tile(xc, ya, a1, 37, yprev),
        tile(xb, yc, b0, 38, xnext), tile(xa, yc, b1, 39, xprev),
    ]

    table = at[...]
    masked_row = me[...]
    squares0 = jnp.sum(table * table, axis=1, keepdims=True)
    squares1 = 2.0 * jnp.sum(table * masked_row, axis=1, keepdims=True) + jnp.sum(masked_row * masked_row)
    empty = jnp.zeros((120, 128), F32)
    base0 = jnp.transpose(jnp.concatenate([jnp.broadcast_to(squares0, (8, 128)), empty], axis=0))[0:1, :]
    base1 = jnp.transpose(jnp.concatenate([jnp.broadcast_to(squares1, (8, 128)), empty], axis=0))[0:1, :]

    t_opp.wait_recv()
    t_fwd = go(ph.at[m2], ph.at[m2], 71, sib)
    whole_group(2).wait_recv()
    whole_group(3).wait_recv()
    t_sib.wait_recv()
    t_fwd.wait_recv()

    extra = ex[...].reshape(512, 128)
    wide_extra = extra.astype(F32)
    masked = wide_extra[:, 8:9]
    e_parts = [(ph[b].reshape(512, 128).astype(F32) * (1.0 - masked)).astype(BF16) for b in range(4)]
    e = jnp.concatenate(e_parts + [extra], axis=1)
    g_all = gl[...]
    g_scaled = jnp.concatenate([g_all[0:512], 2.0 * g_all[512:528], jnp.zeros((112, 128), F32)], axis=0)
    g_high = g_scaled.astype(BF16)
    g_low = (g_scaled - g_high.astype(F32)).astype(BF16)
    products = jnp.dot(e, jnp.concatenate([g_high, g_low], axis=1), preferred_element_type=F32)
    mine = (products[:, 0:128] + products[:, 128:256]) * (ph[m].reshape(512, 128).astype(F32) * (1.0 - masked))
    nb[0] = lax.dot_general(
        jnp.ones((8, 128), F32), mine, NT, precision=lax.Precision.HIGHEST, preferred_element_type=F32)
    n_copies = [
        go(nb.at[0], nb.at[1], 72, opp), go(nb.at[0], nb.at[3], 74, (w, n3)), go(nb.at[0], nb.at[2], 73, sib)]
    own_base = jnp.concatenate([base0, base1, lane8[0:1], jnp.zeros((5, 128), F32)], axis=0)
    base = lax.dot_general(own_base, wide_extra, NT, precision=lax.Precision.HIGHEST, preferred_element_type=F32)
    base = base[0:1] + base[2:3] * base[1:2]

    for k in ends:
        k.wait_recv()
    pad = jnp.zeros((112, 256), BF16)

    def project(j):
        rhs = jnp.concatenate(
            [kf[(2 * j) // 4, (2 * j) % 4], kf[(2 * j + 1) // 4, (2 * j + 1) % 4]], axis=1)
        rhs = jnp.concatenate([rhs, pad], axis=0)
        qkv[:, j * 256:j * 256 + 256] = jnp.dot(e, rhs, preferred_element_type=F32).astype(BF16)

    for j in range(7):
        project(j)
    for k in n_copies:
        k.wait_recv()
    squares = ((nb[0] + nb[1]) + (nb[2] + nb[3])) + base
    scale = lax.rsqrt(jnp.maximum(squares, 0.0) * (1.0 / 5120.0) + 1e-05)
    nb[4] = scale
    sc[...] = jnp.transpose(scale)

    row = lax.broadcasted_iota(jnp.int32, (128, 128), 0)
    col = lax.broadcasted_iota(jnp.int32, (128, 128), 1)
    keep_mask = ((row & 3) == (col & 3)) & ((row & 64) == (col & 64)) & (col <= row)
    bias = jnp.where(keep_mask, 0.0, -1e30)
    bias = jnp.concatenate([bias] * 5, axis=0)

    def group(i, carry):
        rows = pl.ds(pl.multiple_of(i * 128, 128), 128)
        col_scale = nb[4, 0:1, rows]
        row_scale = jnp.concatenate([sc[rows, 0:1] * (1.0 / HEAD**0.5)] * 5, axis=0)
        for h in range(2):
            q = jnp.concatenate(
                [qkv[rows, (h * 5 + g) * 128:(h * 5 + g) * 128 + 128] for g in range(5)], axis=0)
            k = qkv[rows, 1280 + h * 128:1408 + h * 128]
            v = qkv[rows, 1536 + h * 128:1664 + h * 128]
            s = lax.dot_general(q, k, NT, preferred_element_type=F32) * row_scale * col_scale
            s = s + bias
            top = jnp.max(s, axis=1, keepdims=True)
            exps = jnp.exp(s - top)
            total = jnp.sum(exps, axis=1, keepdims=True)
            mixed = jnp.dot((exps * col_scale).astype(BF16), v, preferred_element_type=F32)
            mixed = (mixed / total).astype(BF16)
            for g in range(5):
                out[pl.ds(i * 32, 32), :, (h * 5 + g) * 128:(h * 5 + g) * 128 + 128] = mixed[g * 128:g * 128 + 128].reshape(32, 4, 128)
        return carry

    lax.fori_loop(0, 4, group, 0)

    for k in started:
        k.wait_send()
    for group in range(5):
        whole_group(group).wait_send()


VMEM = pl.BlockSpec(memory_space=pltpu.VMEM)
ANY = pl.BlockSpec(memory_space=pl.ANY)


def shards(
    frames_in, conv_weight, embed_weight, action_table, mask_embed, norm_gain,
    q_weight, k_weight, v_weight, action_ids, token_mask,
):
    attended = pl.pallas_call(
        whole_kernel,
        out_shape=jax.ShapeDtypeStruct((128, 4, 1280), BF16),
        in_specs=[pl.BlockSpec(memory_space=pltpu.SMEM)] + [ANY] * 10,
        out_specs=VMEM,
        scratch_shapes=[
            pltpu.VMEM((2, 16, 16, 128), BF16),
            pltpu.VMEM((8, 5120), F32),
            pltpu.VMEM((1, 5120), F32),
            pltpu.VMEM((1, 5120), F32),
            pltpu.VMEM((80, 1280), BF16),
            pltpu.VMEM((80, 256), BF16),
            pltpu.VMEM((80, 256), BF16),
            pltpu.VMEM((2, 256), jnp.int32),
            pltpu.VMEM((WIN, 128), F32),
            pltpu.VMEM((27, 512, 128), BF16),
            pltpu.VMEM((4, 4, 18, 16, 128), BF16),
            pltpu.VMEM((512, 384), F32),
            pltpu.VMEM((512, 128), F32),
            pltpu.VMEM((4, 16, 8, 128), BF16),
            pltpu.VMEM((4, 16, 8, 128), BF16),
            pltpu.VMEM((4, 16, 8, 128), BF16),
            pltpu.VMEM((4, 16, 8, 128), BF16),
            pltpu.VMEM((4, 4, 4, 8, 128), BF16),
            pltpu.VMEM((4, 4, 4, 4, 8, 128), BF16),
            pltpu.VMEM((16, 80, 128), BF16),
            pltpu.VMEM((DEPTH, 128), BF16),
            pltpu.VMEM((64, 8, DEPTH), BF16),
            pltpu.VMEM((32, DEPTH), BF16),
            pltpu.VMEM((48, 128), F32),
            pltpu.VMEM((4, 48, 128), F32),
            pltpu.VMEM((528, 128), F32),
            pltpu.VMEM((4, 144, 128), BF16),
            pltpu.VMEM((4, 144, 128), BF16),
            pltpu.VMEM((4, 4, 528, 128), BF16),
            pltpu.VMEM((5, 8, 512), F32),
            pltpu.VMEM((512, 8), F32),
            pltpu.VMEM((512, 1792), BF16),
            pltpu.SemaphoreType.DMA((13,)),
            pltpu.SemaphoreType.DMA((75,)),
            pltpu.SemaphoreType.DMA((75,)),
            pltpu.SemaphoreType.DMA((5,)),
            pltpu.SemaphoreType.DMA((5,)),
        ],
        compiler_params=pltpu.CompilerParams(
            collective_id=0, has_side_effects=True, vmem_limit_bytes=60 * 1024 * 1024
        ),
        name="whole",
    )(
        action_ids, frames_in, conv_weight, embed_weight.reshape(16, 8, 5120),
        action_table, mask_embed.reshape(1, 5120), norm_gain.reshape(1, 5120), q_weight, k_weight, v_weight, token_mask,
    )
    return attended.reshape(128, 4, 1, 1280)


def solution(mesh):
    return jax.shard_map(
        shards,
        mesh=mesh,
        in_specs=(
            P("wide", None, None, "narrow"),
            P(None, None, "narrow"),
            P("narrow", None),
            P(),
            P(),
            P(),
            P("wide", "narrow"),
            P("wide", "narrow"),
            P("wide", "narrow"),
            P("wide"),
            P("wide", None),
        ),
        out_specs=P(None, None, "wide", "narrow"),
        check_vma=False,
    )
```

```python
import jax
import jax.numpy as jnp
from jax import lax
from jax.experimental import pallas as pl
from jax.experimental.pallas import tpu as pltpu
from jax.sharding import PartitionSpec as P

MESH = pl.DeviceIdType.MESH
F32 = jnp.float32
BF16 = jnp.bfloat16
HEAD = 128
WIN = 384
DEPTH = 4 * WIN
NT = (((1,), (1,)), ((), ()))


def whole_kernel(
    ids, fr_hbm, cw_hbm, ew_hbm, at_hbm, me_hbm, ga_hbm, qw_hbm, kw_hbm, vw_hbm, tm_hbm,
    out,
    fr, at, me, ga, qw, kw, vw, tm, gc, cw, xr, acc, ge, pieces, qe, xx, qx, ex, ph, ws, wb, fb, sb, gp, gr, gl, ka, kr, kf, nb, sc, qkv,
    lsem, ssem, rsem, psend, precv,
):
    w = lax.axis_index("wide")
    n = lax.axis_index("narrow")
    x, zl, y = w // 16, (w // 4) % 4, w % 4
    zh, c = n // 2, n % 2
    p = x * 4 + y
    n1, n2, n3 = zh * 2 + (1 - c), (1 - zh) * 2 + c, (1 - zh) * 2 + (1 - c)
    m, m1, m2 = c * 2 + zh, (1 - c) * 2 + zh, c * 2 + (1 - zh)
    odd = zl % 2
    start = (zl * 320 // 128) * 128

    def at_plane(px, py):
        return px * 16 + zl * 4 + py

    xs, ys, zs = ([at] + [(at + d) % 4 for d in range(1, 4)] for at in (x, y, zl))

    def zpeer(d):
        return zs[d], (x * 16 + zs[d] * 4 + y, n)

    def ppeer(d):
        px, py = xs[d // 4], ys[d % 4]
        return px * 4 + py, (at_plane(px, py), n)

    sib, opp = (w, n1), (w, n2)
    wnext, wprev = ((w + 1) % 64, n), ((w + 63) % 64, n)
    xa, xc, xb = xs[1:]
    ya, yc, yb = ys[1:]
    xnext, xprev = (at_plane(xa, y), n), (at_plane(xb, y), n)
    ynext, yprev = (at_plane(x, ya), n), (at_plane(x, yb), n)

    def cp(src, dst, slot, dev):
        return pltpu.make_async_remote_copy(
            src_ref=src, dst_ref=dst, send_sem=ssem.at[slot], recv_sem=rsem.at[slot],
            device_id=dev, device_id_type=MESH,
        )

    started = []

    def go(src, dst, slot, dev):
        k = cp(src, dst, slot, dev)
        k.start()
        started.append(k)
        return k

    def pcp(src, dst, group, d, dev):
        return pltpu.make_async_remote_copy(
            src_ref=src, dst_ref=dst, send_sem=psend.at[group], recv_sem=precv.at[group],
            device_id=dev, device_id_type=MESH,
        )

    def plane(make, op):
        for d in range(1, 16):
            op(make(d))

    def begin(k):
        k.start()

    def whole_group(group):
        ref = (wb.at[pl.ds(0, 1200)], fb.at[pl.ds(0, 15)], pieces.at[:, pl.ds(0, 15)], gl.at[pl.ds(0, 480)],
               pieces.at[:, pl.ds(0, 15)])[group]
        return pcp(ref, ref, group, 1, ppeer(1)[1])

    e_loads = []
    for i in range(4):
        e_loads.append(pltpu.make_async_copy(
            ew_hbm.at[:, :, pl.ds(pl.multiple_of(1280 * i + start, 128), WIN)],
            fb.at[pl.ds(m * 16, 16), :, pl.ds(WIN * i, WIN)],
            lsem.at[i],
        ))
        e_loads[-1].start()
    loads = []
    for i, (src, dst) in enumerate((
        (fr_hbm, fr), (ga_hbm, ga), (qw_hbm, qw), (kw_hbm, kw), (vw_hbm, vw), (at_hbm, at), (me_hbm, me), (tm_hbm, tm),
        (cw_hbm, cw),
    )):
        loads.append(pltpu.make_async_copy(src, dst, lsem.at[4 + i]))
        loads[-1].start()
    taps = loads.pop()

    barrier = pltpu.get_barrier_semaphore()

    def greet(dev):
        pl.semaphore_signal(barrier, inc=1, device_id=dev, device_id_type=MESH)

    for dev in (sib, opp, (w, n3), wnext, wprev, zpeer(1)[1], zpeer(2)[1], zpeer(3)[1]):
        greet(dev)

    for d in range(1, 16):
        greet(ppeer(d)[1])

    for i in range(4):
        wb[pl.ds(pl.multiple_of(i * WIN + (1 - odd) * 320, 16), 64), :] = jnp.zeros((64, 128), BF16)
    zero_row = jnp.zeros((4, 4, 1, 16, 128), BF16)
    xr[:, :, 0:1] = zero_row
    xr[:, :, 17:18] = zero_row

    def w_rows(px, py):
        return pl.ds(pl.multiple_of(px * WIN + odd * 64 + py * 80, 16), 80)

    for k in e_loads + loads:
        k.wait()
    pl.semaphore_wait(barrier, 23)

    e_opp = go(fb.at[m * 16 + p], fb.at[m * 16 + p], 11, opp)
    inner = pl.ds(1, 16)
    f_opp = go(fr, xr.at[n, pl.ds(1, 2), inner], 1, opp)
    h_next = go(fr.at[1], xr.at[n, 0, inner], 3, wnext)
    h_prev = go(fr.at[0], xr.at[n, 3, inner], 4, wprev)
    f_sib = go(fr, xr.at[n, pl.ds(1, 2), inner], 0, sib)
    e_sib = go(fb.at[pl.ds(m * 16, 16)], fb.at[pl.ds(m * 16, 16)], 12, sib)

    cols = pl.ds(pl.multiple_of(1280 * x + start, 128), WIN)
    gain = jnp.broadcast_to(ga[:, cols], (8, WIN))
    for i in range(3):
        gc[i * 128:i * 128 + 128] = jnp.transpose(
            jnp.concatenate([gain[:, i * 128:i * 128 + 128], jnp.zeros((120, 128), F32)], axis=0))
    gain = gc[pl.ds(pl.multiple_of(odd * 64 + y * 80, 8), 80), :][:, 0:1]
    for t in range(14):
        source, col = (qw, t) if t < 10 else ((kw, t - 10) if t < 12 else (vw, t - 12))
        ws[t] = (source[:, col * 128:col * 128 + 128].astype(F32) * gain).astype(BF16)
    for t in range(14, 16):
        ws[t] = jnp.zeros((80, 128), BF16)

    def w_copy(d):
        there, dev = ppeer(d)
        return pcp(ws.at[there], wb.at[w_rows(x, y)], 0, d, dev)

    plane(w_copy, begin)
    wb[w_rows(x, y), :] = ws[p]
    xr[n, 1:3, 1:17] = fr[...]

    e_opp.wait_recv()

    def e_copy(d):
        there, dev = ppeer(d)
        return pcp(fb.at[m2 * 16 + p], fb.at[m2 * 16 + p], 1, d, dev)

    plane(e_copy, begin)

    lane = lax.broadcasted_iota(jnp.int32, (4, 128), 1)
    onehot = jnp.concatenate([jnp.where(lane == ids[f], 1.0, 0.0) for f in range(2)], axis=0)
    lane8 = jnp.where(lax.broadcasted_iota(jnp.int32, (8, 128), 1) == 8, 1.0, 0.0)
    masks = jnp.concatenate(
        [tm[f:f + 1, i * 64:i * 64 + 64] for f in range(2) for i in range(4)], axis=0)
    masks = jnp.where(masks == 1, 1.0, 0.0)
    for z in range(4):
        for k in range(16):
            where = (k // 4) * 16 + z * 4 + k % 4
            xx[z, k] = (onehot + masks[:, where:where + 1] * lane8).astype(BF16)
    qx[zl] = xx[zl]
    x_copies = []
    for d in range(1, 4):
        there, dev = zpeer(d)
        x_copies.append(go(xx.at[there], qx.at[zl], 12 + d, dev))

    for i in range(4):
        cols = pl.ds(pl.multiple_of(1280 * i + start, 128), WIN)
        rows = jnp.concatenate([at[:, cols], me[:, cols], jnp.zeros((7, WIN), F32)], axis=0)
        high = rows.astype(BF16)
        sb[0:16, i * WIN:i * WIN + WIN] = high
        sb[16:32, i * WIN:i * WIN + WIN] = (rows - high.astype(F32)).astype(BF16)

    f_opp.wait_recv()
    h2_next = go(xr.at[n2, 2, inner], xr.at[n2, 0, inner], 5, wnext)
    h2_prev = go(xr.at[n2, 1, inner], xr.at[n2, 3, inner], 6, wprev)
    f_fwd = go(xr.at[n2, pl.ds(1, 2), inner], xr.at[n2, pl.ds(1, 2), inner], 2, sib)
    h_next.wait_recv()
    h_prev.wait_recv()
    s_copies = [
        go(xr.at[n, 0, inner], xr.at[n, 0, inner], 7, sib), go(xr.at[n, 3, inner], xr.at[n, 3, inner], 8, sib)]

    whole_group(1).wait_recv()
    e_fwd = go(fb.at[pl.ds(m2 * 16, 16)], fb.at[pl.ds(m2 * 16, 16)], 10, sib)
    for k in x_copies:
        k.wait_recv()

    def x_copy(d):
        there, dev = ppeer(d)
        return pcp(qx.at[:, there], ex.at[x, :, y], 2, d, dev)

    plane(x_copy, begin)
    for z in range(4):
        ex[x, z, y] = qx[z, p]

    def taps_of(dt):
        def tap(dh, carry):
            total = acc[...]
            lhs = jnp.concatenate(
                [xr[b, dt:dt + 2, pl.ds(dh, 16)].reshape(512, 128) for b in range(4)], axis=1)
            rhs = jnp.concatenate([cw[dt * 9 + dh * 3 + dw] for dw in range(3)], axis=1)
            acc[...] = total + jnp.dot(lhs, rhs, preferred_element_type=F32)
            return carry
        lax.fori_loop(0, 3, tap, 0)

    f_sib.wait_recv()
    f_fwd.wait_recv()

    h2_next.wait_recv()
    h2_prev.wait_recv()
    s_copies += [
        go(xr.at[n2, 0, inner], xr.at[n2, 0, inner], 9, sib), go(xr.at[n2, 3, inner], xr.at[n2, 3, inner], 25, sib)]

    whole_group(0).wait_recv()
    e_sib.wait_recv()
    e_fwd.wait_recv()

    part = jnp.dot(fb[...].reshape(512, DEPTH), wb[...], preferred_element_type=F32)
    for b in range(4):
        ka[b, 0:128] = part[b * 128:b * 128 + 128].astype(BF16)
    both = jnp.dot(sb[...], wb[...], preferred_element_type=F32)
    for b in range(4):
        ka[b, 128:144] = (both[0:16] + both[16:32]).astype(BF16)
    k_copies = []
    for d in range(1, 4):
        there, dev = zpeer(d)
        k_copies.append(go(ka.at[there], kr.at[zl], 18 + d, dev))
    kr[zl] = ka[zl]

    where = lax.broadcasted_iota(jnp.int32, (1, WIN), 1) + (1 - odd) * 64
    valid = jnp.where(where >= 64, jnp.where(where < 384, 1.0, 0.0), 0.0)
    valid = jnp.concatenate([valid] * 4, axis=1)
    block = (fb[pl.ds(m * 16, 16)].reshape(128, DEPTH).astype(F32) * valid).astype(BF16)
    rows = jnp.concatenate([fb[pl.ds(p * 4, 4)].reshape(32, DEPTH), sb[...]], axis=0)
    both = lax.dot_general(rows, block, NT, preferred_element_type=F32)
    gp[0:32] = both[0:32]
    gp[32:48] = both[32:48] + both[48:64]
    g_copies = []
    for d in range(1, 4):
        there, dev = zpeer(d)
        g_copies.append(go(gp, gr.at[zl], 15 + d, dev))
    gr[zl] = gp[...]

    taps.wait()
    acc[...] = jnp.zeros(acc.shape, F32)
    taps_of(1)

    for k in k_copies:
        k.wait_recv()
    ksum = (kr[0].astype(F32) + kr[1].astype(F32)) + (kr[2].astype(F32) + kr[3].astype(F32))

    def quarter():
        return pl.ds(pl.multiple_of(zl * 128, 16), 128)

    kf[x, y, quarter(), :] = ksum[0:128].astype(BF16)
    kf[x, y, 512:528, :] = ksum[128:144].astype(BF16)
    q_copies = []
    for d in range(1, 4):
        there, dev = zpeer(d)
        q_copies.append(go(kf.at[x, y, quarter()], kf.at[x, y, quarter()], 21 + d, dev))

    for k in g_copies:
        k.wait_recv()
    gsum = (gr[0] + gr[1]) + (gr[2] + gr[3])

    def g_rows():
        return pl.ds(pl.multiple_of(p * 32, 8), 32)

    gl[g_rows(), :] = gsum[0:32]
    gl[512:528] = gsum[32:48]

    def g_copy(d):
        there, dev = ppeer(d)
        return pcp(gl.at[g_rows()], gl.at[g_rows()], 3, d, dev)

    plane(g_copy, begin)

    for k in s_copies:
        k.wait_recv()
    for k in s_copies:
        k.wait_send()
        started[:] = [other for other in started if other is not k]

    @pl.when(w == 0)
    def _():
        xr[:, 0, 1:17] = jnp.zeros((4, 16, 16, 128), BF16)

    @pl.when(w == 63)
    def _():
        xr[:, 3, 1:17] = jnp.zeros((4, 16, 16, 128), BF16)

    taps_of(0)

    taps_of(2)

    half_a, half_b = pl.ds(0, 256), pl.ds(256, 272)
    a0, a1, b0, b1 = pl.ds(0, 128), pl.ds(128, 128), pl.ds(256, 144), pl.ds(400, 128)

    def tile(tx, ty, rows, slot, dev):
        return go(kf.at[tx, ty, rows], kf.at[tx, ty, rows], 30 + slot, dev)

    for k in q_copies:
        k.wait_recv()
    near = [
        tile(x, y, half_a, 0, xnext), tile(x, y, half_a, 1, xprev),
        tile(x, y, half_b, 2, ynext), tile(x, y, half_b, 3, yprev),
    ]
    column = lax.broadcasted_iota(jnp.int32, (512, 128), 0) & 15
    left = jnp.where(column == 0, 0.0, pltpu.roll(acc[:, 0:128], 1, 0))
    right = jnp.where(column == 15, 0.0, pltpu.roll(acc[:, 256:384], 511, 0))
    ge[...] = jax.nn.gelu(acc[:, 128:256] + left + right)
    for z in range(4):
        for k in range(16):
            here = (k // 4) * 16 + z * 4 + k % 4
            pieces[z, k] = ge[pl.ds(here, 8, stride=64), :].astype(BF16)
    p_copies = []
    for d in range(1, 4):
        there, dev = zpeer(d)
        p_copies.append(go(pieces.at[there], qe.at[zl], 25 + d, dev))
    qe[zl] = pieces[zl]

    for k in near:
        k.wait_recv()
    far = [
        tile(xb, y, a0, 8, xnext), tile(xa, y, a1, 9, xprev),
        tile(x, yb, b0, 10, ynext), tile(x, ya, b1, 11, yprev),
    ]
    for k in p_copies:
        k.wait_recv()

    def p_copy(d):
        there, dev = ppeer(d)
        return pcp(qe.at[:, there], ph.at[m, x, :, y], 4, d, dev)

    plane(p_copy, begin)
    for z in range(4):
        ph[m, x, z, y] = qe[z, p]

    own = [
        tile(x, y, half_a, 4, ynext), tile(x, y, half_a, 5, yprev),
        tile(x, y, half_b, 6, xnext), tile(x, y, half_b, 7, xprev),
    ]

    turned = []
    for i, (tx, ty) in enumerate(((xb, yb), (xa, ya))):
        turned += [
            tile(tx, y, half_a, 12 + 4 * i, ynext), tile(tx, y, half_a, 13 + 4 * i, yprev),
            tile(x, ty, half_b, 14 + 4 * i, xnext), tile(x, ty, half_b, 15 + 4 * i, xprev),
        ]

    whole_group(4).wait_recv()
    t_opp = go(ph.at[m], ph.at[m], 29, opp)
    t_sib = go(ph.at[m], ph.at[m], 70, sib)

    for k in own:
        k.wait_recv()
    ends = [
        tile(x, yb, a0, 20, ynext), tile(x, ya, a1, 21, yprev),
        tile(xb, y, b0, 22, xnext), tile(xa, y, b1, 23, xprev),
    ]
    for k in far:
        k.wait_recv()
    across = [
        tile(xc, y, half_a, 24, ynext), tile(xc, y, half_a, 25, yprev),
        tile(x, yc, half_b, 26, xnext), tile(x, yc, half_b, 27, xprev),
    ]

    for k in turned:
        k.wait_recv()
    ends += [
        tile(xb, yb, a0, 28, ynext), tile(xb, ya, a1, 29, yprev),
        tile(xa, yb, a0, 30, ynext), tile(xa, ya, a1, 31, yprev),
        tile(xb, yb, b0, 32, xnext), tile(xa, yb, b1, 33, xprev),
        tile(xb, ya, b0, 34, xnext), tile(xa, ya, b1, 35, xprev),
    ]

    for k in across:
        k.wait_recv()
    ends += [
        tile(xc, yb, a0, 36, ynext), tile(xc, ya, a1, 37, yprev),
        tile(xb, yc, b0, 38, xnext), tile(xa, yc, b1, 39, xprev),
    ]

    table = at[...]
    masked_row = me[...]
    squares0 = jnp.sum(table * table, axis=1, keepdims=True)
    squares1 = 2.0 * jnp.sum(table * masked_row, axis=1, keepdims=True) + jnp.sum(masked_row * masked_row)
    empty = jnp.zeros((120, 128), F32)
    base0 = jnp.transpose(jnp.concatenate([jnp.broadcast_to(squares0, (8, 128)), empty], axis=0))[0:1, :]
    base1 = jnp.transpose(jnp.concatenate([jnp.broadcast_to(squares1, (8, 128)), empty], axis=0))[0:1, :]

    t_opp.wait_recv()
    t_fwd = go(ph.at[m2], ph.at[m2], 71, sib)
    whole_group(2).wait_recv()
    whole_group(3).wait_recv()
    t_sib.wait_recv()
    t_fwd.wait_recv()

    extra = ex[...].reshape(512, 128)
    wide_extra = extra.astype(F32)
    masked = wide_extra[:, 8:9]
    e_parts = [(ph[b].reshape(512, 128).astype(F32) * (1.0 - masked)).astype(BF16) for b in range(4)]
    e = jnp.concatenate(e_parts + [extra], axis=1)
    g_all = gl[...]
    g_scaled = jnp.concatenate([g_all[0:512], 2.0 * g_all[512:528], jnp.zeros((112, 128), F32)], axis=0)
    g_high = g_scaled.astype(BF16)
    g_low = (g_scaled - g_high.astype(F32)).astype(BF16)
    products = jnp.dot(e, jnp.concatenate([g_high, g_low], axis=1), preferred_element_type=F32)
    mine = (products[:, 0:128] + products[:, 128:256]) * (ph[m].reshape(512, 128).astype(F32) * (1.0 - masked))
    mine_high = mine.astype(BF16)
    mine_both = jnp.concatenate([mine_high, (mine - mine_high.astype(F32)).astype(BF16)], axis=1)
    nb[0] = lax.dot_general(jnp.ones((8, 256), BF16), mine_both, NT, preferred_element_type=F32)
    n_copies = [
        go(nb.at[0], nb.at[1], 72, opp), go(nb.at[0], nb.at[3], 74, (w, n3)), go(nb.at[0], nb.at[2], 73, sib)]
    own_base = jnp.concatenate([base0, base1, lane8[0:1], jnp.zeros((5, 128), F32)], axis=0)
    base = lax.dot_general(own_base, wide_extra, NT, precision=lax.Precision.HIGHEST, preferred_element_type=F32)
    base = base[0:1] + base[2:3] * base[1:2]

    for k in ends:
        k.wait_recv()
    pad = jnp.zeros((112, 256), BF16)

    def project(j):
        rhs = jnp.concatenate(
            [kf[(2 * j) // 4, (2 * j) % 4], kf[(2 * j + 1) // 4, (2 * j + 1) % 4]], axis=1)
        rhs = jnp.concatenate([rhs, pad], axis=0)
        qkv[:, j * 256:j * 256 + 256] = jnp.dot(e, rhs, preferred_element_type=F32).astype(BF16)

    for j in range(7):
        project(j)
    for k in n_copies:
        k.wait_recv()
    squares = ((nb[0] + nb[1]) + (nb[2] + nb[3])) + base
    scale = lax.rsqrt(jnp.maximum(squares, 0.0) * (1.0 / 5120.0) + 1e-05)
    nb[4] = scale
    sc[...] = jnp.transpose(scale)

    row = lax.broadcasted_iota(jnp.int32, (128, 128), 0)
    col = lax.broadcasted_iota(jnp.int32, (128, 128), 1)
    keep_mask = ((row & 3) == (col & 3)) & ((row & 64) == (col & 64)) & (col <= row)
    bias = jnp.where(keep_mask, 0.0, -1e30)
    bias = jnp.concatenate([bias] * 5, axis=0)

    def group(i, carry):
        rows = pl.ds(pl.multiple_of(i * 128, 128), 128)
        col_scale = nb[4, 0:1, rows]
        row_scale = jnp.concatenate([sc[rows, 0:1] * (1.0 / HEAD**0.5)] * 5, axis=0)
        for h in range(2):
            q = jnp.concatenate(
                [qkv[rows, (h * 5 + g) * 128:(h * 5 + g) * 128 + 128] for g in range(5)], axis=0)
            k = qkv[rows, 1280 + h * 128:1408 + h * 128]
            v = qkv[rows, 1536 + h * 128:1664 + h * 128]
            s = lax.dot_general(q, k, NT, preferred_element_type=F32) * row_scale * col_scale
            s = s + bias
            top = jnp.max(s, axis=1, keepdims=True)
            exps = jnp.exp(s - top)
            total = jnp.sum(exps, axis=1, keepdims=True)
            mixed = jnp.dot((exps * col_scale).astype(BF16), v, preferred_element_type=F32)
            mixed = (mixed / total).astype(BF16)
            for g in range(5):
                out[pl.ds(i * 32, 32), :, (h * 5 + g) * 128:(h * 5 + g) * 128 + 128] = mixed[g * 128:g * 128 + 128].reshape(32, 4, 128)
        return carry

    lax.fori_loop(0, 4, group, 0)

    for k in started:
        k.wait_send()
    for group in range(5):
        whole_group(group).wait_send()


VMEM = pl.BlockSpec(memory_space=pltpu.VMEM)
ANY = pl.BlockSpec(memory_space=pl.ANY)


def shards(
    frames_in, conv_weight, embed_weight, action_table, mask_embed, norm_gain,
    q_weight, k_weight, v_weight, action_ids, token_mask,
):
    attended = pl.pallas_call(
        whole_kernel,
        out_shape=jax.ShapeDtypeStruct((128, 4, 1280), BF16),
        in_specs=[pl.BlockSpec(memory_space=pltpu.SMEM)] + [ANY] * 10,
        out_specs=VMEM,
        scratch_shapes=[
            pltpu.VMEM((2, 16, 16, 128), BF16),
            pltpu.VMEM((8, 5120), F32),
            pltpu.VMEM((1, 5120), F32),
            pltpu.VMEM((1, 5120), F32),
            pltpu.VMEM((80, 1280), BF16),
            pltpu.VMEM((80, 256), BF16),
            pltpu.VMEM((80, 256), BF16),
            pltpu.VMEM((2, 256), jnp.int32),
            pltpu.VMEM((WIN, 128), F32),
            pltpu.VMEM((27, 512, 128), BF16),
            pltpu.VMEM((4, 4, 18, 16, 128), BF16),
            pltpu.VMEM((512, 384), F32),
            pltpu.VMEM((512, 128), F32),
            pltpu.VMEM((4, 16, 8, 128), BF16),
            pltpu.VMEM((4, 16, 8, 128), BF16),
            pltpu.VMEM((4, 16, 8, 128), BF16),
            pltpu.VMEM((4, 16, 8, 128), BF16),
            pltpu.VMEM((4, 4, 4, 8, 128), BF16),
            pltpu.VMEM((4, 4, 4, 4, 8, 128), BF16),
            pltpu.VMEM((16, 80, 128), BF16),
            pltpu.VMEM((DEPTH, 128), BF16),
            pltpu.VMEM((64, 8, DEPTH), BF16),
            pltpu.VMEM((32, DEPTH), BF16),
            pltpu.VMEM((48, 128), F32),
            pltpu.VMEM((4, 48, 128), F32),
            pltpu.VMEM((528, 128), F32),
            pltpu.VMEM((4, 144, 128), BF16),
            pltpu.VMEM((4, 144, 128), BF16),
            pltpu.VMEM((4, 4, 528, 128), BF16),
            pltpu.VMEM((5, 8, 512), F32),
            pltpu.VMEM((512, 8), F32),
            pltpu.VMEM((512, 1792), BF16),
            pltpu.SemaphoreType.DMA((13,)),
            pltpu.SemaphoreType.DMA((75,)),
            pltpu.SemaphoreType.DMA((75,)),
            pltpu.SemaphoreType.DMA((5,)),
            pltpu.SemaphoreType.DMA((5,)),
        ],
        compiler_params=pltpu.CompilerParams(
            collective_id=0, has_side_effects=True, vmem_limit_bytes=60 * 1024 * 1024
        ),
        name="whole",
    )(
        action_ids, frames_in, conv_weight, embed_weight.reshape(16, 8, 5120),
        action_table, mask_embed.reshape(1, 5120), norm_gain.reshape(1, 5120), q_weight, k_weight, v_weight, token_mask,
    )
    return attended.reshape(128, 4, 1, 1280)


def solution(mesh):
    return jax.shard_map(
        shards,
        mesh=mesh,
        in_specs=(
            P("wide", None, None, "narrow"),
            P(None, None, "narrow"),
            P("narrow", None),
            P(),
            P(),
            P(),
            P("wide", "narrow"),
            P("wide", "narrow"),
            P("wide", "narrow"),
            P("wide"),
            P("wide", None),
        ),
        out_specs=P(None, None, "wide", "narrow"),
        check_vma=False,
    )
```
